256 devices in a mesh: row: 16 (over z, y_lo), col: 16 (over x, y_hi, core).
Axes of the slice: x: 4, y: 4 (y_hi: 2, y_lo: 2; y = y_hi * 2 + y_lo), z: 8, core: 2. Of those that a mesh axis runs over, the one named last changes fastest.
Arguments:
- left_proj: bfloat16 [512, 512, 128], P('row', 'col'), may hold values from -6 to 6
- right_proj: bfloat16 [512, 512, 128], P('col', 'row'), may hold values from -6 to 6
- gate: bfloat16 [512, 512, 128], P('row', 'col'), may hold values from -8 to 8
- out_weight: bfloat16 [128, 128], replicated, may hold values from -0.5 to 0.5
- grad_out: bfloat16 [512, 512, 128], P('row', 'col'), may hold values from -6 to 6
Outputs:
- grad_left: bfloat16 [512, 512, 128], P('row', 'col')
- grad_right: bfloat16 [512, 512, 128], P('col', 'row')
- grad_gate: bfloat16 [512, 512, 128], P('row', 'col')
- grad_weight: float32 [128, 128], replicated
The draws below stay inside these ranges and needn't reach their ends.
All inputs are finite; a program needn't handle non-finite values.
Results may differ from the reference program's by a relative error of at most 0.0057.
Values may be sent and summed in bfloat16 or wider, within the bound.
No kernel may reach another device: no remote copies, remote signals or barrier semaphores. Data moves between devices by JAX's collectives and lax.ppermute only.
A program may use at most 128 MiB of HBM per device.

```python
import jax
import jax.numpy as jnp
from jax import lax

CH = 128
CZ = 128
TOKENS = 512


def shard_levels(stream_key, extent, shards, low, largest):
    gain = 1.0
    for axis_at, parts in shards:
        steps = jax.random.uniform(jax.random.fold_in(jax.random.fold_in(stream_key, 6), axis_at), (parts,), jnp.float32, low / len(shards), largest / len(shards))
        gain = gain * jnp.repeat(jnp.exp(steps), extent[axis_at] // parts).reshape((-1,) + (1,) * (len(extent) - 1 - axis_at))
    return gain


def normal_values(stream_key, dims, deviation, most, shards=(), dtype=jnp.bfloat16):
    values = jax.random.normal(stream_key, dims, jnp.float32) * deviation
    if len(shards) > 0:
        values = shard_levels(stream_key, dims, shards, -0.22, 0.18) * values
    return jnp.clip(values, min=-most, max=most).astype(dtype)


def setup_inputs(seed: int = 0) -> dict:
    seeds = jax.random.split(jax.random.key(seed), 6)
    return {
        "left_proj": normal_values(seeds[0], (TOKENS, TOKENS, CH), 1.0, 6.0, ((0, 16), (1, 16))),
        "right_proj": normal_values(seeds[1], (TOKENS, TOKENS, CH), 1.0, 6.0, ((0, 16), (1, 16))),
        "gate": normal_values(seeds[2], (TOKENS, TOKENS, CZ), 2.0, 8.0, ((0, 16), (1, 16))),
        "out_weight": normal_values(seeds[3], (CH, CZ), CH ** -0.5, 0.5),
        "grad_out": normal_values(seeds[4], (TOKENS, TOKENS, CZ), 1.0, 6.0, ((0, 16), (1, 16))),
    }


def reference(left_proj, right_proj, gate, out_weight, grad_out):
    left_f = left_proj.astype(jnp.float32)
    right_f = right_proj.astype(jnp.float32)
    pair = jnp.einsum('ikc,jkc->ijc', left_f, right_f)
    average = lax.optimization_barrier(jnp.mean(pair, axis=-1, keepdims=True))
    centered = pair - average
    variance = lax.optimization_barrier(jnp.mean(centered * centered, axis=-1, keepdims=True))
    inv_std = lax.rsqrt(variance + 1e-05)
    normed = centered * inv_std
    normed_half = normed.astype(jnp.bfloat16)
    gate_prob = jax.nn.sigmoid(gate.astype(jnp.float32))
    upstream = grad_out.astype(jnp.float32)
    gated_grad = (upstream * gate_prob).astype(jnp.bfloat16)
    weight_f = out_weight.astype(jnp.float32)
    projected = jnp.einsum('ijc,cd->ijd', normed_half.astype(jnp.float32), weight_f)
    grad_gate = (upstream * projected * gate_prob * (1.0 - gate_prob)).astype(jnp.bfloat16)
    grad_weight = jnp.einsum('ijc,ijd->cd', normed_half.astype(jnp.float32), gated_grad.astype(jnp.float32)) / TOKENS
    grad_normed = jnp.einsum('ijd,cd->ijc', gated_grad.astype(jnp.float32), weight_f)
    mean_one = lax.optimization_barrier(jnp.mean(grad_normed, axis=-1, keepdims=True))
    mean_two = lax.optimization_barrier(jnp.mean(grad_normed * normed, axis=-1, keepdims=True))
    grad_pair = ((grad_normed - mean_one - normed * mean_two) * inv_std).astype(jnp.bfloat16)
    pair_f = grad_pair.astype(jnp.float32)
    grad_left = jnp.einsum('ijc,jkc->ikc', pair_f, right_f).astype(jnp.bfloat16)
    grad_right = jnp.einsum('ijc,ikc->jkc', pair_f, left_f).astype(jnp.bfloat16)
    return (grad_left, grad_right, grad_gate, grad_weight)
```

```python
import jax
import jax.numpy as jnp
from jax import lax
from jax.experimental import pallas as pl
from jax.experimental.pallas import tpu as pltpu
from jax.sharding import PartitionSpec as P

F32 = jnp.float32
BF16 = jnp.bfloat16
BOTH = ("row", "col")
PARAMS = pltpu.CompilerParams(vmem_limit_bytes=32 * 1024 * 1024)
NT = (((1,), (1,)), ((), ()))
TN = (((0,), (0,)), ((), ()))


def chunk_transpose(parts):
    lane = lax.broadcasted_iota(jnp.int32, parts[0].shape, 1)
    low = lane < 64
    even = (lane & 32) == 0
    turn = lambda x, by: pltpu.roll(x, by, 1)
    y0, y1, y2, y3 = parts
    a0 = jnp.where(low, y0, turn(y2, 64))
    a2 = jnp.where(low, turn(y0, 64), y2)
    a1 = jnp.where(low, y1, turn(y3, 64))
    a3 = jnp.where(low, turn(y1, 64), y3)
    return [
        jnp.where(even, a0, turn(a1, 32)),
        jnp.where(even, turn(a0, 96), a1),
        jnp.where(even, a2, turn(a3, 32)),
        jnp.where(even, turn(a2, 96), a3),
    ]


def pack_kernel(left_ref, right_ref, out_ref, slabs):
    for side, ref in enumerate((left_ref, right_ref)):
        for s in range(8):
            slab = ref[pl.ds(s * 128, 128), :].astype(F32)
            slabs[:, side * 8 + s, :] = slab.T
    out_ref[...] = slabs[...].astype(BF16)


def unpack_kernel(in_ref, left_ref, right_ref, slabs):
    slabs[...] = in_ref[...].astype(F32)
    for side, ref in enumerate((left_ref, right_ref)):
        for s in range(8):
            ref[pl.ds(s * 128, 128), :] = slabs[:, side * 8 + s, :].T.astype(BF16)


def pair_kernel(core_ref, own_ref, other_ref, a_ref, b_ref, out_ref, va, vb, nat, prod):
    core = core_ref[0]

    @pl.when(core == 0)
    def _():
        va[...] = own_ref[...].astype(F32)
        vb[...] = other_ref[...].astype(F32)

    @pl.when(core == 1)
    def _():
        vb[...] = own_ref[...].astype(F32)
        va[...] = other_ref[...].astype(F32)

    for g in range(4):
        for rc in range(4):
            parts = [va[pl.ds(4 * rc, 4), 4 * g + t].reshape(32, 128) for t in range(4)]
            for lo, part in enumerate(chunk_transpose(parts)):
                a_ref[pl.ds(lo * 128 + rc * 32, 32), pl.ds(g * 128, 128)] = part.astype(BF16)
            parts = [vb[4 * g + t, pl.ds(4 * rc, 4)].reshape(32, 128) for t in range(4)]
            for lo, part in enumerate(chunk_transpose(parts)):
                nat[g, pl.ds(rc * 128 + lo, 32, stride=4), :] = part
    for g in range(4):
        b_ref[:, pl.ds(g * 128, 128)] = nat[g].astype(BF16)
    for g in range(4):
        rows = pl.ds(g * 128, 128)
        prod[g] = lax.dot_general(a_ref[...], b_ref[rows, :], NT, preferred_element_type=F32)
    for half in range(2):

        @pl.when(core == half)
        def _():
            for g in range(4):
                for rc in range(4):
                    parts = [prod[g, pl.ds(lo * 128 + rc * 32, 32), :] for lo in range(4)]
                    for t, part in enumerate(chunk_transpose(parts)):
                        out_ref[pl.ds(4 * rc, 4), 4 * g + t] = part.reshape(4, 8, 128)[
                            :, 4 * half : 4 * half + 4
                        ]


def norm_kernel(pair_ref, gate_ref, grad_ref, weight_ref, gate_out, weight_out, out_ref, slabs):
    weight = weight_ref[...]
    total = jnp.zeros((128, 128), F32)
    for s in range(8):
        rows = pl.ds(s * 128, 128)
        pair = pair_ref[:, s, :].T
        average = jnp.mean(pair, axis=-1, keepdims=True)
        centered = pair - average
        variance = jnp.mean(centered * centered, axis=-1, keepdims=True)
        inv_std = lax.rsqrt(variance + 1e-05)
        normed = centered * inv_std
        normed_half = normed.astype(BF16)
        gate_prob = jax.nn.sigmoid(gate_ref[rows, :].astype(F32))
        upstream = grad_ref[rows, :].astype(F32)
        gated = upstream * gate_prob
        gated_grad = gated.astype(BF16)
        projected = jnp.dot(normed_half, weight, preferred_element_type=F32)
        gate_out[rows, :] = (gated * projected * (1.0 - gate_prob)).astype(BF16)
        total += lax.dot_general(normed_half, gated_grad, TN, preferred_element_type=F32)
        grad_normed = lax.dot_general(gated_grad, weight, NT, preferred_element_type=F32)
        mean_one = jnp.mean(grad_normed, axis=-1, keepdims=True)
        mean_two = jnp.mean(grad_normed * normed, axis=-1, keepdims=True)
        grad_pair = (grad_normed - mean_one - normed * mean_two) * inv_std
        slabs[:, s, :] = grad_pair.T
    weight_out[...] = total * (1.0 / 512.0)
    out_ref[...] = slabs[...].astype(BF16)


def grad_kernel(core_ref, own_ref, other_ref, a_ref, b_ref, out_ref, raw, gp, prod):
    core = core_ref[0]

    @pl.when(core == 0)
    def _():
        raw[:, :, 0:4, :] = own_ref[...].astype(F32)
        raw[:, :, 4:8, :] = other_ref[...].astype(F32)

    @pl.when(core == 1)
    def _():
        raw[:, :, 0:4, :] = other_ref[...].astype(F32)
        raw[:, :, 4:8, :] = own_ref[...].astype(F32)

    for g in range(4):
        for rc in range(4):
            parts = [raw[pl.ds(4 * rc, 4), 4 * g + t].reshape(32, 128) for t in range(4)]
            for lo, part in enumerate(chunk_transpose(parts)):
                gp[pl.ds(lo * 128 + rc * 32, 32), pl.ds(g * 128, 128)] = part.astype(BF16)

    @pl.when(core == 0)
    def _():
        for g in range(4):
            prod[g] = jnp.dot(gp[...], b_ref[:, pl.ds(g * 128, 128)], preferred_element_type=F32)
            for rc in range(4):
                parts = [prod[g, pl.ds(lo * 128 + rc * 32, 32), :] for lo in range(4)]
                for t, part in enumerate(chunk_transpose(parts)):
                    out_ref[pl.ds(4 * rc, 4), 4 * g + t] = part.reshape(4, 8, 128).astype(BF16)

    @pl.when(core == 1)
    def _():
        for g in range(4):
            prod[g] = lax.dot_general(
                gp[...], a_ref[:, pl.ds(g * 128, 128)], TN, preferred_element_type=F32
            )
            for qc in range(4):
                parts = [
                    prod[g, pl.ds(qc * 128 + lo, 32, stride=4), :] for lo in range(4)
                ]
                for t, part in enumerate(chunk_transpose(parts)):
                    out_ref[4 * g + t, pl.ds(4 * qc, 4)] = part.reshape(4, 8, 128).astype(BF16)


VM = pl.BlockSpec(memory_space=pltpu.VMEM)
SM = pl.BlockSpec(memory_space=pltpu.SMEM)


def call(kernel, outs, ins, scratch, name):
    return pl.pallas_call(
        kernel,
        out_shape=[jax.ShapeDtypeStruct(s, d) for s, d in outs],
        in_specs=ins,
        out_specs=[VM] * len(outs),
        scratch_shapes=[pltpu.VMEM(s, d) for s, d in scratch],
        compiler_params=PARAMS,
        name=name,
    )


def exchange(x, axis):
    return lax.all_to_all(x, axis, 0, 0, tiled=True)


def other_core(x):
    return lax.ppermute(x, "col", [(i, i ^ 1) for i in range(16)])


def local(left_proj, right_proj, gate, out_weight, grad_out):
    core = (lax.axis_index("col") % 2).astype(jnp.int32).reshape(1)
    (packed,) = call(pack_kernel, [((128, 16, 128), BF16)], [VM] * 2, [((128, 16, 128), F32)], "pack")(
        left_proj.reshape(1024, 128), right_proj.reshape(1024, 128)
    )
    own = exchange(packed.reshape(256, 8, 128), BOTH)
    other = other_core(own)
    block = (16, 16, 8, 128)
    a, b, pair = call(
        pair_kernel,
        [((512, 512), BF16), ((512, 512), BF16), ((16, 16, 4, 128), F32)],
        [SM, VM, VM],
        [(block, F32), (block, F32), ((4, 512, 128), F32), ((4, 512, 128), F32)],
        "pair",
    )(core, own.reshape(block), other.reshape(block))
    pair = exchange(pair.reshape(256, 4, 128), BOTH).reshape(128, 8, 128)
    grad_gate, weight_terms, grad_pair = call(
        norm_kernel,
        [((1024, 128), BF16), ((128, 128), F32), ((128, 8, 128), BF16)],
        [VM] * 4,
        [((128, 8, 128), F32)],
        "norm",
    )(pair, gate.reshape(1024, 128), grad_out.reshape(1024, 128), out_weight)
    own = exchange(grad_pair.reshape(256, 4, 128), BOTH)
    other = other_core(own)
    half = (16, 16, 4, 128)
    (grads,) = call(
        grad_kernel,
        [(block, BF16)],
        [SM, VM, VM, VM, VM],
        [(block, F32), ((512, 512), BF16), ((4, 512, 128), F32)],
        "grads",
    )(core, own.reshape(half), other.reshape(half), a, b)
    grads = exchange(grads.reshape(256, 8, 128), BOTH).reshape(128, 16, 128)
    grad_left, grad_right = call(
        unpack_kernel, [((1024, 128), BF16)] * 2, [VM], [((128, 16, 128), F32)], "unpack"
    )(grads)
    part = exchange(weight_terms.reshape(16, 8, 128), "col").sum(0)
    part = exchange(jnp.broadcast_to(part[None], (16, 8, 128)), "row").sum(0)
    grad_weight = exchange(jnp.broadcast_to(part[None], (16, 8, 128)), "col").reshape(128, 128)
    shape = (32, 32, 128)
    return grad_left.reshape(shape), grad_right.reshape(shape), grad_gate.reshape(shape), grad_weight


def solution(mesh):
    return jax.shard_map(
        local,
        mesh=mesh,
        in_specs=(
            P("row", "col", None),
            P("col", "row", None),
            P("row", "col", None),
            P(),
            P("row", "col", None),
        ),
        out_specs=(P("row", "col", None), P("col", "row", None), P("row", "col", None), P()),
        check_vma=False,
    )
```

```python
import jax
import jax.numpy as jnp
from jax import lax
from jax.experimental import pallas as pl
from jax.experimental.pallas import tpu as pltpu
from jax.sharding import PartitionSpec as P

F32 = jnp.float32
BF16 = jnp.bfloat16
BOTH = ("row", "col")
PARAMS = pltpu.CompilerParams(vmem_limit_bytes=32 * 1024 * 1024)
NT = (((1,), (1,)), ((), ()))
TN = (((0,), (0,)), ((), ()))


def chunk_transpose(parts):
    lane = lax.broadcasted_iota(jnp.int32, parts[0].shape, 1)
    low = lane < 64
    even = (lane & 32) == 0
    turn = lambda x, by: pltpu.roll(x, by, 1)
    y0, y1, y2, y3 = parts
    a0 = jnp.where(low, y0, turn(y2, 64))
    a2 = jnp.where(low, turn(y0, 64), y2)
    a1 = jnp.where(low, y1, turn(y3, 64))
    a3 = jnp.where(low, turn(y1, 64), y3)
    return [
        jnp.where(even, a0, turn(a1, 32)),
        jnp.where(even, turn(a0, 96), a1),
        jnp.where(even, a2, turn(a3, 32)),
        jnp.where(even, turn(a2, 96), a3),
    ]


def pack_kernel(left_ref, right_ref, out_ref, slabs):
    for side, ref in enumerate((left_ref, right_ref)):
        for s in range(8):
            slab = ref[pl.ds(s * 128, 128), :].astype(F32)
            slabs[:, side * 8 + s, :] = slab.T
    out_ref[...] = slabs[...].astype(BF16)


def split_halves(x):
    high = x.astype(BF16).astype(F32)
    return high, (x - high).astype(BF16).astype(F32)


def unpack_kernel(in_ref, left_ref, right_ref, weight_ref, slabs):
    for side, ref in enumerate((left_ref, right_ref)):
        for pair in range(5):
            slabs[:, 2 * pair : 2 * pair + 2, :] = in_ref[:, side, pair].astype(F32)
        for s in range(8):
            ref[pl.ds(s * 128, 128), :] = slabs[:, s, :].T.astype(BF16)
    weight_ref[...] = slabs[:, 8, :] + slabs[:, 9, :]


def pair_kernel(core_ref, own_ref, other_ref, a_ref, b_ref, out_ref, va, vb, nat, prod):
    core = core_ref[0]

    @pl.when(core == 0)
    def _():
        va[...] = own_ref[...].astype(F32)
        vb[...] = other_ref[...].astype(F32)

    @pl.when(core == 1)
    def _():
        vb[...] = own_ref[...].astype(F32)
        va[...] = other_ref[...].astype(F32)

    for g in range(4):
        for rc in range(4):
            parts = [va[pl.ds(4 * rc, 4), 4 * g + t].reshape(32, 128) for t in range(4)]
            for lo, part in enumerate(chunk_transpose(parts)):
                a_ref[pl.ds(lo * 128 + rc * 32, 32), pl.ds(g * 128, 128)] = part.astype(BF16)
            parts = [vb[4 * g + t, pl.ds(4 * rc, 4)].reshape(32, 128) for t in range(4)]
            for lo, part in enumerate(chunk_transpose(parts)):
                nat[g, pl.ds(rc * 128 + lo, 32, stride=4), :] = part
    for g in range(4):
        b_ref[:, pl.ds(g * 128, 128)] = nat[g].astype(BF16)
    for g in range(4):
        rows = pl.ds(g * 128, 128)
        prod[g] = lax.dot_general(a_ref[...], b_ref[rows, :], NT, preferred_element_type=F32)
    for half in range(2):

        @pl.when(core == half)
        def _():
            for g in range(4):
                for rc in range(4):
                    parts = [prod[g, pl.ds(lo * 128 + rc * 32, 32), :] for lo in range(4)]
                    for t, part in enumerate(chunk_transpose(parts)):
                        out_ref[pl.ds(4 * rc, 4), 4 * g + t] = part.reshape(4, 8, 128)[
                            :, 4 * half : 4 * half + 4
                        ]


def norm_kernel(pair_ref, gate_ref, grad_ref, weight_ref, gate_out, out_ref, slabs):
    weight = weight_ref[...]
    total = jnp.zeros((128, 128), F32)
    for s in range(8):
        rows = pl.ds(s * 128, 128)
        pair = pair_ref[:, s, :].T
        average = jnp.mean(pair, axis=-1, keepdims=True)
        centered = pair - average
        variance = jnp.mean(centered * centered, axis=-1, keepdims=True)
        inv_std = lax.rsqrt(variance + 1e-05)
        normed = centered * inv_std
        normed_half = normed.astype(BF16)
        gate_prob = jax.nn.sigmoid(gate_ref[rows, :].astype(F32))
        upstream = grad_ref[rows, :].astype(F32)
        gated = upstream * gate_prob
        gated_grad = gated.astype(BF16)
        projected = jnp.dot(normed_half, weight, preferred_element_type=F32)
        gate_out[rows, :] = (gated * projected * (1.0 - gate_prob)).astype(BF16)
        total += lax.dot_general(normed_half, gated_grad, TN, preferred_element_type=F32)
        grad_normed = lax.dot_general(gated_grad, weight, NT, preferred_element_type=F32)
        mean_one = jnp.mean(grad_normed, axis=-1, keepdims=True)
        mean_two = jnp.mean(grad_normed * normed, axis=-1, keepdims=True)
        grad_pair = (grad_normed - mean_one - normed * mean_two) * inv_std
        slabs[:, s, :] = grad_pair.T
    for half in range(2):
        for pair in range(2):
            at = 4 * half + 2 * pair
            out_ref[:, half, pair] = slabs[:, at : at + 2, :].astype(BF16)
    high, rest = split_halves(total * (1.0 / 512.0))
    slabs[:, 0, :] = high
    slabs[:, 1, :] = rest
    terms = slabs[:, 0:2, :].astype(BF16)
    out_ref[:, 0, 2] = terms
    out_ref[:, 1, 2] = terms


def grad_kernel(core_ref, own_ref, other_ref, a_ref, b_ref, out_ref, raw, gp, prod):
    core = core_ref[0]

    @pl.when(core == 0)
    def _():
        for pair in range(2):
            raw[:, :, 2 * pair : 2 * pair + 2, :] = own_ref[:, :, pair].astype(F32)
            raw[:, :, 4 + 2 * pair : 6 + 2 * pair, :] = other_ref[:, :, pair].astype(F32)

    @pl.when(core == 1)
    def _():
        for pair in range(2):
            raw[:, :, 2 * pair : 2 * pair + 2, :] = other_ref[:, :, pair].astype(F32)
            raw[:, :, 4 + 2 * pair : 6 + 2 * pair, :] = own_ref[:, :, pair].astype(F32)

    total = jnp.sum(own_ref[:, :, 2].astype(F32).reshape(256, 2, 128), axis=0)
    high, rest = split_halves(jnp.sum(total, axis=0, keepdims=True))
    terms = jnp.concatenate([high, rest], axis=0).astype(BF16)
    out_ref[:, :, 4] = jnp.broadcast_to(terms[None, None], (16, 16, 2, 128))

    for g in range(4):
        for rc in range(4):
            parts = [raw[pl.ds(4 * rc, 4), 4 * g + t].reshape(32, 128) for t in range(4)]
            for lo, part in enumerate(chunk_transpose(parts)):
                gp[pl.ds(lo * 128 + rc * 32, 32), pl.ds(g * 128, 128)] = part.astype(BF16)

    @pl.when(core == 0)
    def _():
        for g in range(4):
            prod[g] = jnp.dot(gp[...], b_ref[:, pl.ds(g * 128, 128)], preferred_element_type=F32)
            for rc in range(4):
                parts = [prod[g, pl.ds(lo * 128 + rc * 32, 32), :] for lo in range(4)]
                for t, part in enumerate(chunk_transpose(parts)):
                    block = part.reshape(4, 8, 128)
                    for pair in range(4):
                        out_ref[pl.ds(4 * rc, 4), 4 * g + t, pair] = block[
                            :, 2 * pair : 2 * pair + 2
                        ].astype(BF16)

    @pl.when(core == 1)
    def _():
        for g in range(4):
            prod[g] = lax.dot_general(
                gp[...], a_ref[:, pl.ds(g * 128, 128)], TN, preferred_element_type=F32
            )
            for qc in range(4):
                parts = [
                    prod[g, pl.ds(qc * 128 + lo, 32, stride=4), :] for lo in range(4)
                ]
                for t, part in enumerate(chunk_transpose(parts)):
                    block = part.reshape(4, 8, 128)
                    for pair in range(4):
                        out_ref[4 * g + t, pl.ds(4 * qc, 4), pair] = block[
                            :, 2 * pair : 2 * pair + 2
                        ].astype(BF16)


VM = pl.BlockSpec(memory_space=pltpu.VMEM)
SM = pl.BlockSpec(memory_space=pltpu.SMEM)


def call(kernel, outs, ins, scratch, name):
    return pl.pallas_call(
        kernel,
        out_shape=[jax.ShapeDtypeStruct(s, d) for s, d in outs],
        in_specs=ins,
        out_specs=[VM] * len(outs),
        scratch_shapes=[pltpu.VMEM(s, d) for s, d in scratch],
        compiler_params=PARAMS,
        name=name,
    )


def exchange(x, axis):
    return lax.all_to_all(x, axis, 0, 0, tiled=True)


def other_core(x):
    return lax.ppermute(x, "col", [(i, i ^ 1) for i in range(16)])


def local(left_proj, right_proj, gate, out_weight, grad_out):
    core = (lax.axis_index("col") % 2).astype(jnp.int32).reshape(1)
    (packed,) = call(pack_kernel, [((128, 16, 128), BF16)], [VM] * 2, [((128, 16, 128), F32)], "pack")(
        left_proj.reshape(1024, 128), right_proj.reshape(1024, 128)
    )
    own = exchange(packed.reshape(256, 8, 128), BOTH)
    other = other_core(own)
    block = (16, 16, 8, 128)
    a, b, pair = call(
        pair_kernel,
        [((512, 512), BF16), ((512, 512), BF16), ((16, 16, 4, 128), F32)],
        [SM, VM, VM],
        [(block, F32), (block, F32), ((4, 512, 128), F32), ((4, 512, 128), F32)],
        "pair",
    )(core, own.reshape(block), other.reshape(block))
    pair = exchange(pair.reshape(256, 4, 128), BOTH).reshape(128, 8, 128)
    grad_gate, grad_pair = call(
        norm_kernel,
        [((1024, 128), BF16), ((128, 2, 3, 2, 128), BF16)],
        [VM] * 4,
        [((128, 8, 128), F32)],
        "norm",
    )(pair, gate.reshape(1024, 128), grad_out.reshape(1024, 128), out_weight)
    own = exchange(grad_pair.reshape(256, 3, 2, 128), BOTH)
    other = other_core(own)
    half = (16, 16, 3, 2, 128)
    (grads,) = call(
        grad_kernel,
        [((16, 16, 5, 2, 128), BF16)],
        [SM, VM, VM, VM, VM],
        [(block, F32), ((512, 512), BF16), ((4, 512, 128), F32)],
        "grads",
    )(core, own.reshape(half), other.reshape(half), a, b)
    grads = exchange(grads.reshape(256, 5, 2, 128), BOTH).reshape(128, 2, 5, 2, 128)
    grad_left, grad_right, grad_weight = call(
        unpack_kernel,
        [((1024, 128), BF16), ((1024, 128), BF16), ((128, 128), F32)],
        [VM],
        [((128, 10, 128), F32)],
        "unpack",
    )(grads)
    shape = (32, 32, 128)
    return grad_left.reshape(shape), grad_right.reshape(shape), grad_gate.reshape(shape), grad_weight


def solution(mesh):
    return jax.shard_map(
        local,
        mesh=mesh,
        in_specs=(
            P("row", "col", None),
            P("col", "row", None),
            P("row", "col", None),
            P(),
            P("row", "col", None),
        ),
        out_specs=(P("row", "col", None), P("col", "row", None), P("row", "col", None), P()),
        check_vma=False,
    )
```

```python
import jax
import jax.numpy as jnp
from jax import lax
from jax.experimental import pallas as pl
from jax.experimental.pallas import tpu as pltpu
from jax.sharding import PartitionSpec as P

F32 = jnp.float32
BF16 = jnp.bfloat16
PARAMS = pltpu.CompilerParams(vmem_limit_bytes=32 * 1024 * 1024)
NT = (((1,), (1,)), ((), ()))
TN = (((0,), (0,)), ((), ()))

SAME_CORE = [[row * 16 + col for row in range(16) for col in range(core, 16, 2)] for core in (0, 1)]


def chunk_transpose(parts):
    lane = lax.broadcasted_iota(jnp.int32, parts[0].shape, 1)
    low = lane < 64
    even = (lane & 32) == 0
    turn = lambda x, by: pltpu.roll(x, by, 1)
    y0, y1, y2, y3 = parts
    a0 = jnp.where(low, y0, turn(y2, 64))
    a2 = jnp.where(low, turn(y0, 64), y2)
    a1 = jnp.where(low, y1, turn(y3, 64))
    a3 = jnp.where(low, turn(y1, 64), y3)
    return [
        jnp.where(even, a0, turn(a1, 32)),
        jnp.where(even, turn(a0, 96), a1),
        jnp.where(even, a2, turn(a3, 32)),
        jnp.where(even, turn(a2, 96), a3),
    ]


def split_halves(x):
    high = x.astype(BF16).astype(F32)
    return high, (x - high).astype(BF16).astype(F32)


def pack_kernel(core_ref, left_ref, right_ref, out_ref, slabs):
    for side, ref in enumerate((left_ref, right_ref)):
        for s in range(8):
            slab = ref[pl.ds(s * 128, 128), :].astype(F32)
            slabs[:, side * 8 + s, :] = slab.T
    out_ref[...] = slabs[...].astype(BF16)


def unpack_kernel(in_ref, left_ref, right_ref, weight_ref, slabs):
    slabs[...] = in_ref[...].astype(F32)
    for side, ref in enumerate((left_ref, right_ref)):
        for s in range(8):
            slab = slabs[pl.ds(side * 8 + s, 128, stride=18), :]
            ref[pl.ds(s * 128, 128), :] = slab.T.astype(BF16)
    weight_ref[...] = slabs[pl.ds(16, 128, stride=18), :] + slabs[pl.ds(17, 128, stride=18), :]


def order_kernel(core_ref, in_ref, a_ref, keep_ref, send_ref, raw, nat):
    core = core_ref[0]
    raw[...] = in_ref[...].astype(F32)
    for g in range(2):
        for rc in range(4):
            parts = [raw[pl.ds(4 * rc, 4), 4 * g + t, 0:8].reshape(32, 128) for t in range(4)]
            for lo, part in enumerate(chunk_transpose(parts)):
                a_ref[pl.ds(lo * 128 + rc * 32, 32), pl.ds(g * 128, 128)] = part.astype(BF16)
    for which, ref in enumerate((keep_ref, send_ref)):
        parity = core if which == 0 else 1 - core
        for g in range(2):
            for qc in range(2):
                parts = [
                    raw[2 * (4 * g + t) + parity, pl.ds(4 * qc, 4), 8:16].reshape(32, 128)
                    for t in range(4)
                ]
                for lo, part in enumerate(chunk_transpose(parts)):
                    nat[2 * which + g, pl.ds(qc * 128 + lo, 32, stride=4), :] = part
            ref[:, pl.ds(g * 128, 128)] = nat[2 * which + g].astype(BF16)


def pair_kernel(a_ref, other_ref, keep_ref, send_ref, out_ref, prod):
    value = lax.dot_general(a_ref[...], keep_ref[...], NT, preferred_element_type=F32)
    value += lax.dot_general(other_ref[...], send_ref[...], NT, preferred_element_type=F32)
    for g in range(2):
        prod[g] = value[:, g * 128 : (g + 1) * 128]
    for g in range(2):
        for rc in range(4):
            parts = [prod[g, pl.ds(lo * 128 + rc * 32, 32), :] for lo in range(4)]
            for t, part in enumerate(chunk_transpose(parts)):
                out_ref[pl.ds(4 * rc, 4), 4 * g + t] = part.reshape(4, 8, 128)


def norm_kernel(pair_ref, gate_ref, grad_ref, weight_ref, gate_out, out_ref, slabs):
    weight = weight_ref[...]
    total = jnp.zeros((128, 128), F32)
    for s in range(8):
        rows = pl.ds(s * 128, 128)
        pair = pair_ref[pl.ds(s, 128, stride=8), :]
        average = jnp.mean(pair, axis=0, keepdims=True)
        centered = pair - average
        variance = jnp.mean(centered * centered, axis=0, keepdims=True)
        inv_std = lax.rsqrt(variance + 1e-05)
        normed = centered * inv_std
        normed_half = normed.astype(BF16)
        gate_prob = jax.nn.sigmoid(gate_ref[rows, :].astype(F32))
        upstream = grad_ref[rows, :].astype(F32)
        gated = upstream * gate_prob
        gated_grad = gated.astype(BF16)
        projected = lax.dot_general(normed_half, weight, TN, preferred_element_type=F32)
        gate_out[rows, :] = (gated * projected * (1.0 - gate_prob)).astype(BF16)
        total += jnp.dot(normed_half, gated_grad, preferred_element_type=F32)
        grad_normed = lax.dot_general(weight, gated_grad, NT, preferred_element_type=F32)
        mean_one = jnp.mean(grad_normed, axis=0, keepdims=True)
        mean_two = jnp.mean(grad_normed * normed, axis=0, keepdims=True)
        grad_pair = (grad_normed - mean_one - normed * mean_two) * inv_std
        slabs[pl.ds(s, 128, stride=10), :] = grad_pair
    high, rest = split_halves(total * (1.0 / 512.0))
    slabs[pl.ds(8, 128, stride=10), :] = high
    slabs[pl.ds(9, 128, stride=10), :] = rest
    out_ref[...] = slabs[...].astype(BF16)


def grad_kernel(core_ref, own_ref, far_ref, a_ref, other_ref, keep_ref, got_ref, out_ref, raw, gp, prod, flat, out):
    core = core_ref[0]
    for which, ref in enumerate((own_ref, far_ref)):
        raw[which] = ref[...].astype(F32)
        for g in range(2):
            for rc in range(4):
                parts = [
                    jnp.concatenate(
                        [raw[which, pl.ds((8 * r + 4 * g + t) * 10, 8), :] for r in range(4 * rc, 4 * rc + 4)]
                    )
                    for t in range(4)
                ]
                for lo, part in enumerate(chunk_transpose(parts)):
                    gp[which, pl.ds(lo * 128 + rc * 32, 32), pl.ds(g * 128, 128)] = part.astype(BF16)

    terms = [raw[which, pl.ds(8 + row, 128, stride=10), :] for which in range(2) for row in range(2)]
    sums = [jnp.sum(term, axis=0, keepdims=True) for term in terms]
    high, rest = split_halves((sums[0] + sums[1]) + (sums[2] + sums[3]))
    out[pl.ds(16, 128, stride=18), :] = jnp.broadcast_to(high, (128, 128))
    out[pl.ds(17, 128, stride=18), :] = jnp.broadcast_to(rest, (128, 128))

    value = jnp.dot(gp[0], keep_ref[...], preferred_element_type=F32)
    value += jnp.dot(gp[1], got_ref[...], preferred_element_type=F32)
    for g in range(2):
        prod[g] = value[:, g * 128 : (g + 1) * 128]
    for g in range(2):
        for rc in range(4):
            parts = [prod[g, pl.ds(lo * 128 + rc * 32, 32), :] for lo in range(4)]
            for t, part in enumerate(chunk_transpose(parts)):
                for u in range(4):
                    first = ((4 * rc + u) * 8 + 4 * g + t) * 18
                    out[pl.ds(first, 8), :] = part[8 * u : 8 * u + 8]

    for which, ref in enumerate((a_ref, other_ref)):
        parity = core if which == 0 else 1 - core
        value = lax.dot_general(gp[0], ref[...], TN, preferred_element_type=F32)
        for g in range(2):
            flat[2 * which + g] = value[:, g * 128 : (g + 1) * 128]
        for g in range(2):
            for qc in range(2):
                parts = [
                    flat[2 * which + g, pl.ds(qc * 128 + lo, 32, stride=4), :] for lo in range(4)
                ]
                for t, part in enumerate(chunk_transpose(parts)):
                    for u in range(4):
                        first = parity * 144 + (4 * g + t) * 288 + (4 * qc + u) * 18 + 8
                        out[pl.ds(first, 8), :] = part[8 * u : 8 * u + 8]
    out_ref[...] = out[...].astype(BF16)


VM = pl.BlockSpec(memory_space=pltpu.VMEM)
SM = pl.BlockSpec(memory_space=pltpu.SMEM)


def call(kernel, outs, ins, scratch, name):
    return pl.pallas_call(
        kernel,
        out_shape=[jax.ShapeDtypeStruct(s, d) for s, d in outs],
        in_specs=ins,
        out_specs=[VM] * len(outs),
        scratch_shapes=[pltpu.VMEM(s, d) for s, d in scratch],
        compiler_params=PARAMS,
        name=name,
    )


def exchange(x):
    return lax.all_to_all(x, ("row", "col"), 0, 0, axis_index_groups=SAME_CORE, tiled=True)


def other_core(x):
    return lax.ppermute(x, "col", [(i, i ^ 1) for i in range(16)])


def local(left_proj, right_proj, gate, out_weight, grad_out):
    core = (lax.axis_index("col") & 1).astype(jnp.int32).reshape(1)
    (packed,) = call(pack_kernel, [((128, 16, 128), BF16)], [SM, VM, VM], [((128, 16, 128), F32)], "pack")(
        core, left_proj.reshape(1024, 128), right_proj.reshape(1024, 128)
    )
    blocks = exchange(packed)
    a, keep, send = call(
        order_kernel,
        [((512, 256), BF16), ((256, 256), BF16), ((256, 256), BF16)],
        [SM, VM],
        [((16, 8, 16, 128), F32), ((4, 256, 128), F32)],
        "order",
    )(core, blocks.reshape(16, 8, 16, 128))
    other = other_core(a)
    got = other_core(send)
    (pair,) = call(pair_kernel, [((16, 8, 8, 128), F32)], [VM] * 4, [((2, 512, 128), F32)], "pair")(
        a, other, keep, send
    )
    pair = exchange(pair.reshape(128, 8, 128))
    grad_gate, grad_pair = call(
        norm_kernel,
        [((1024, 128), BF16), ((1280, 128), BF16)],
        [VM] * 4,
        [((1280, 128), F32)],
        "norm",
    )(pair.reshape(1024, 128), gate.reshape(1024, 128), grad_out.reshape(1024, 128), out_weight)
    own = exchange(grad_pair.reshape(128, 5, 2, 128))
    far = other_core(own)
    (grads,) = call(
        grad_kernel,
        [((2304, 128), BF16)],
        [SM] + [VM] * 6,
        [
            ((2, 1280, 128), F32),
            ((2, 512, 256), BF16),
            ((2, 512, 128), F32),
            ((4, 256, 128), F32),
            ((2304, 128), F32),
        ],
        "grads",
    )(core, own.reshape(1280, 128), far.reshape(1280, 128), a, other, keep, got)
    grads = exchange(grads.reshape(128, 9, 2, 128))
    grad_left, grad_right, grad_weight = call(
        unpack_kernel,
        [((1024, 128), BF16), ((1024, 128), BF16), ((128, 128), F32)],
        [VM],
        [((2304, 128), F32)],
        "unpack",
    )(grads.reshape(2304, 128))
    shape = (32, 32, 128)
    return grad_left.reshape(shape), grad_right.reshape(shape), grad_gate.reshape(shape), grad_weight


def solution(mesh):
    return jax.shard_map(
        local,
        mesh=mesh,
        in_specs=(
            P("row", "col", None),
            P("col", "row", None),
            P("row", "col", None),
            P(),
            P("row", "col", None),
        ),
        out_specs=(P("row", "col", None), P("col", "row", None), P("row", "col", None), P()),
        check_vma=False,
    )
```

```python
import jax
import jax.numpy as jnp
from jax import lax
from jax.experimental import pallas as pl
from jax.experimental.pallas import tpu as pltpu
from jax.sharding import PartitionSpec as P

F32 = jnp.float32
BF16 = jnp.bfloat16
PARAMS = pltpu.CompilerParams(vmem_limit_bytes=32 * 1024 * 1024)
NT = (((1,), (1,)), ((), ()))
TN = (((0,), (0,)), ((), ()))

SAME_CORE = [[row * 16 + col for row in range(16) for col in range(core, 16, 2)] for core in (0, 1)]


def chunk_transpose(parts):
    lane = lax.broadcasted_iota(jnp.int32, parts[0].shape, 1)
    low = lane < 64
    even = (lane & 32) == 0
    turn = lambda x, by: pltpu.roll(x, by, 1)
    y0, y1, y2, y3 = parts
    a0 = jnp.where(low, y0, turn(y2, 64))
    a2 = jnp.where(low, turn(y0, 64), y2)
    a1 = jnp.where(low, y1, turn(y3, 64))
    a3 = jnp.where(low, turn(y1, 64), y3)
    return [
        jnp.where(even, a0, turn(a1, 32)),
        jnp.where(even, turn(a0, 96), a1),
        jnp.where(even, a2, turn(a3, 32)),
        jnp.where(even, turn(a2, 96), a3),
    ]


def split_halves(x):
    high = x.astype(BF16).astype(F32)
    return high, (x - high).astype(BF16).astype(F32)


def pack_kernel(core_ref, in_ref, out_ref, slabs):
    for side in range(2):
        for s in range(8):
            slab = in_ref[pl.ds(side * 1024 + s * 128, 128), :].astype(F32)
            slabs[:, side * 8 + s, :] = slab.T
    out_ref[...] = slabs[...].astype(BF16)


def unpack_kernel(in_ref, left_ref, right_ref, weight_ref, slabs):
    slabs[...] = in_ref[...].astype(F32)
    for side, ref in enumerate((left_ref, right_ref)):
        for s in range(8):
            slab = slabs[pl.ds(side * 8 + s, 128, stride=18), :]
            ref[pl.ds(s * 128, 128), :] = slab.T.astype(BF16)
    weight_ref[...] = slabs[pl.ds(16, 128, stride=18), :] + slabs[pl.ds(17, 128, stride=18), :]


def left_order_kernel(in_ref, a_ref, raw):
    raw[...] = in_ref[:, :, 0:8].astype(F32)
    for g in range(2):
        for rc in range(4):
            parts = [raw[pl.ds(4 * rc, 4), 4 * g + t].reshape(32, 128) for t in range(4)]
            for lo, part in enumerate(chunk_transpose(parts)):
                a_ref[pl.ds(lo * 128 + rc * 32, 32), pl.ds(g * 128, 128)] = part.astype(BF16)


def right_order_kernel(core_ref, in_ref, keep_ref, send_ref, raw, nat):
    core = core_ref[0]
    raw[...] = in_ref[:, :, 8:16].astype(F32)
    for which, ref in enumerate((keep_ref, send_ref)):
        parity = core if which == 0 else 1 - core
        for g in range(2):
            for qc in range(2):
                parts = [
                    raw[2 * (4 * g + t) + parity, pl.ds(4 * qc, 4)].reshape(32, 128)
                    for t in range(4)
                ]
                for lo, part in enumerate(chunk_transpose(parts)):
                    nat[2 * which + g, pl.ds(qc * 128 + lo, 32, stride=4), :] = part
            ref[:, pl.ds(g * 128, 128)] = nat[2 * which + g].astype(BF16)


def pair_kernel(a_ref, other_ref, keep_ref, send_ref, out_ref, prod):
    value = lax.dot_general(a_ref[...], keep_ref[...], NT, preferred_element_type=F32)
    value += lax.dot_general(other_ref[...], send_ref[...], NT, preferred_element_type=F32)
    for g in range(2):
        prod[g] = value[:, g * 128 : (g + 1) * 128]
    for g in range(2):
        for rc in range(4):
            parts = [prod[g, pl.ds(lo * 128 + rc * 32, 32), :] for lo in range(4)]
            for t, part in enumerate(chunk_transpose(parts)):
                out_ref[pl.ds(4 * rc, 4), 4 * g + t] = part.reshape(4, 8, 128)


def norm_kernel(pair_ref, gate_ref, grad_ref, weight_ref, gate_out, out_ref, slabs):
    weight = weight_ref[...]
    total = jnp.zeros((128, 128), F32)
    for s in range(8):
        rows = pl.ds(s * 128, 128)
        pair = pair_ref[pl.ds(s, 128, stride=8), :]
        average = jnp.mean(pair, axis=0, keepdims=True)
        centered = pair - average
        variance = jnp.mean(centered * centered, axis=0, keepdims=True)
        inv_std = lax.rsqrt(variance + 1e-05)
        normed = centered * inv_std
        normed_half = normed.astype(BF16)
        gate_prob = jax.nn.sigmoid(gate_ref[rows, :].astype(F32))
        upstream = grad_ref[rows, :].astype(F32)
        gated = upstream * gate_prob
        gated_grad = gated.astype(BF16)
        projected = lax.dot_general(normed_half, weight, TN, preferred_element_type=F32)
        gate_out[rows, :] = (gated * projected * (1.0 - gate_prob)).astype(BF16)
        total += jnp.dot(normed_half, gated_grad, preferred_element_type=F32)
        grad_normed = lax.dot_general(weight, gated_grad, NT, preferred_element_type=F32)
        mean_one = jnp.mean(grad_normed, axis=0, keepdims=True)
        mean_two = jnp.mean(grad_normed * normed, axis=0, keepdims=True)
        grad_pair = (grad_normed - mean_one - normed * mean_two) * inv_std
        slabs[pl.ds(s, 128, stride=10), :] = grad_pair
    high, rest = split_halves(total * (1.0 / 512.0))
    slabs[pl.ds(8, 128, stride=10), :] = high
    slabs[pl.ds(9, 128, stride=10), :] = rest
    out_ref[...] = slabs[...].astype(BF16)


def half_order(ref, raw, gp):
    raw[...] = ref[...].astype(F32)
    for g in range(2):
        for rc in range(4):
            parts = [
                jnp.concatenate(
                    [raw[pl.ds((8 * r + 4 * g + t) * 10, 8), :] for r in range(4 * rc, 4 * rc + 4)]
                )
                for t in range(4)
            ]
            for lo, part in enumerate(chunk_transpose(parts)):
                gp[pl.ds(lo * 128 + rc * 32, 32), pl.ds(g * 128, 128)] = part.astype(BF16)
    terms = [raw[pl.ds(8 + row, 128, stride=10), :] for row in range(2)]
    return jnp.sum(terms[0], axis=0, keepdims=True) + jnp.sum(terms[1], axis=0, keepdims=True)


def right_kernel(core_ref, own_ref, a_ref, other_ref, gp_ref, sum_ref, out_ref, raw, flat):
    core = core_ref[0]
    sum_ref[...] = jnp.broadcast_to(half_order(own_ref, raw, gp_ref), (8, 128))
    turned = gp_ref[...].T
    for which, ref in enumerate((a_ref, other_ref)):
        parity = core if which == 0 else 1 - core
        value = jnp.dot(turned, ref[...], preferred_element_type=F32)
        for g in range(2):
            flat[2 * which + g] = value[:, g * 128 : (g + 1) * 128]
        for g in range(2):
            for qc in range(2):
                parts = [
                    flat[2 * which + g, pl.ds(qc * 128 + lo, 32, stride=4), :] for lo in range(4)
                ]
                for t, part in enumerate(chunk_transpose(parts)):
                    where = (2 * (4 * g + t) + parity, pl.ds(4 * qc, 4))
                    out_ref[where] = part.reshape(4, 8, 128).astype(BF16)


def left_kernel(far_ref, gp_ref, keep_ref, got_ref, sum_ref, right_ref, out_ref, raw, gp, prod, out):
    total = half_order(far_ref, raw, gp) + sum_ref[0:1, :]
    high, rest = split_halves(total)
    out[pl.ds(16, 128, stride=18), :] = jnp.broadcast_to(high, (128, 128))
    out[pl.ds(17, 128, stride=18), :] = jnp.broadcast_to(rest, (128, 128))
    value = jnp.dot(gp_ref[...], keep_ref[...], preferred_element_type=F32)
    value += jnp.dot(gp[...], got_ref[...], preferred_element_type=F32)
    for g in range(2):
        prod[g] = value[:, g * 128 : (g + 1) * 128]
    for g in range(2):
        for rc in range(4):
            parts = [prod[g, pl.ds(lo * 128 + rc * 32, 32), :] for lo in range(4)]
            for t, part in enumerate(chunk_transpose(parts)):
                for u in range(4):
                    at = (4 * rc + u) * 8 + 4 * g + t
                    out[pl.ds(at * 18, 8), :] = part[8 * u : 8 * u + 8]
                    out[pl.ds(at * 18 + 8, 8), :] = right_ref[4 * rc + u, 4 * g + t].astype(F32)
    out_ref[...] = out[...].astype(BF16)


VM = pl.BlockSpec(memory_space=pltpu.VMEM)
SM = pl.BlockSpec(memory_space=pltpu.SMEM)


def call(kernel, outs, ins, scratch, name, us=1):
    return pl.pallas_call(
        kernel,
        out_shape=[jax.ShapeDtypeStruct(s, d) for s, d in outs],
        in_specs=ins,
        out_specs=[VM] * len(outs),
        scratch_shapes=[pltpu.VMEM(s, d) for s, d in scratch],
        compiler_params=PARAMS,
        cost_estimate=pl.CostEstimate(flops=0, bytes_accessed=3_000_000 * us, transcendentals=0),
        name=name,
    )


def exchange(x):
    return lax.all_to_all(x, ("row", "col"), 0, 0, axis_index_groups=SAME_CORE, tiled=True)


def other_core(x):
    return lax.ppermute(x, "col", [(i, i ^ 1) for i in range(16)])


def local(left_proj, right_proj, gate, out_weight, grad_out):
    core = (lax.axis_index("col") & 1).astype(jnp.int32).reshape(1)
    sides = jnp.concatenate([left_proj.reshape(1024, 128), right_proj.reshape(1024, 128)])
    (packed,) = call(
        pack_kernel, [((128, 16, 128), BF16)], [SM, VM], [((128, 16, 128), F32)], "pack"
    )(core, sides)
    blocks = exchange(packed).reshape(16, 8, 16, 128)
    (a,) = call(
        left_order_kernel, [((512, 256), BF16)], [VM], [((16, 8, 8, 128), F32)], "left_order"
    )(blocks)
    other = other_core(a)
    keep, send = call(
        right_order_kernel,
        [((256, 256), BF16), ((256, 256), BF16)],
        [SM, VM],
        [((16, 8, 8, 128), F32), ((4, 256, 128), F32)],
        "right_order",
    )(core, blocks)
    got = other_core(send)
    (pair,) = call(
        pair_kernel, [((16, 8, 8, 128), F32)], [VM] * 4, [((2, 512, 128), F32)], "pair"
    )(a, other, keep, send)
    pair = exchange(pair.reshape(128, 8, 128))
    grad_gate, grad_pair = call(
        norm_kernel,
        [((1024, 128), BF16), ((1280, 128), BF16)],
        [VM] * 4,
        [((1280, 128), F32)],
        "norm",
    )(pair.reshape(1024, 128), gate.reshape(1024, 128), grad_out.reshape(1024, 128), out_weight)
    own = exchange(grad_pair.reshape(128, 5, 2, 128))
    far = other_core(own)
    half, total, right = call(
        right_kernel,
        [((512, 256), BF16), ((8, 128), F32), ((16, 8, 8, 128), BF16)],
        [SM] + [VM] * 3,
        [((1280, 128), F32), ((4, 256, 128), F32)],
        "right",
    )(core, own.reshape(1280, 128), a, other)
    (grads,) = call(
        left_kernel,
        [((2304, 128), BF16)],
        [VM] * 6,
        [((1280, 128), F32), ((512, 256), BF16), ((2, 512, 128), F32), ((2304, 128), F32)],
        "left",
    )(far.reshape(1280, 128), half, keep, got, total, right)
    grads = exchange(grads.reshape(128, 9, 2, 128))
    grad_left, grad_right, grad_weight = call(
        unpack_kernel,
        [((1024, 128), BF16), ((1024, 128), BF16), ((128, 128), F32)],
        [VM],
        [((2304, 128), F32)],
        "unpack",
    )(grads.reshape(2304, 128))
    shape = (32, 32, 128)
    return grad_left.reshape(shape), grad_right.reshape(shape), grad_gate.reshape(shape), grad_weight


def solution(mesh):
    return jax.shard_map(
        local,
        mesh=mesh,
        in_specs=(
            P("row", "col", None),
            P("col", "row", None),
            P("row", "col", None),
            P(),
            P("row", "col", None),
        ),
        out_specs=(P("row", "col", None), P("col", "row", None), P("row", "col", None), P()),
        check_vma=False,
    )
```

```python
import functools

import jax
import jax.numpy as jnp
from jax import lax
from jax.experimental import pallas as pl
from jax.experimental.pallas import tpu as pltpu
from jax.sharding import PartitionSpec as P

F32 = jnp.float32
BF16 = jnp.bfloat16
PARAMS = pltpu.CompilerParams(vmem_limit_bytes=32 * 1024 * 1024)
NT = (((1,), (1,)), ((), ()))
TN = (((0,), (0,)), ((), ()))
FLOOR = 1e-07

SAME_CORE = [[row * 16 + col for row in range(16) for col in range(core, 16, 2)] for core in (0, 1)]


def chunk_transpose(parts):
    lane = lax.broadcasted_iota(jnp.int32, parts[0].shape, 1)
    low = lane < 64
    even = (lane & 32) == 0
    turn = lambda x, by: pltpu.roll(x, by, 1)
    y0, y1, y2, y3 = parts
    a0 = jnp.where(low, y0, turn(y2, 64))
    a2 = jnp.where(low, turn(y0, 64), y2)
    a1 = jnp.where(low, y1, turn(y3, 64))
    a3 = jnp.where(low, turn(y1, 64), y3)
    return [
        jnp.where(even, a0, turn(a1, 32)),
        jnp.where(even, turn(a0, 96), a1),
        jnp.where(even, a2, turn(a3, 32)),
        jnp.where(even, turn(a2, 96), a3),
    ]


def split_halves(x):
    high = x.astype(BF16).astype(F32)
    return high, (x - high).astype(BF16).astype(F32)


def pack_kernel(core_ref, in_ref, out_ref, slabs):
    for side in range(2):
        for s in range(8):
            slab = in_ref[pl.ds(side * 1024 + s * 128, 128), :].astype(F32)
            slabs[:, side * 8 + s, :] = slab.T
    out_ref[...] = slabs[...].astype(BF16)


def unpack_kernel(in_ref, left_ref, right_ref, weight_ref, slabs):
    slabs[...] = in_ref[...].astype(F32)
    for side, ref in enumerate((left_ref, right_ref)):
        for s in range(8):
            slab = slabs[pl.ds(side * 8 + s, 128, stride=18), :]
            ref[pl.ds(s * 128, 128), :] = slab.T.astype(BF16)
    weight_ref[...] = slabs[pl.ds(16, 128, stride=18), :] + slabs[pl.ds(17, 128, stride=18), :]


def left_order_kernel(in_ref, a_ref, raw):
    raw[...] = in_ref[:, :, 0:8].astype(F32)
    for g in range(2):
        for rc in range(4):
            parts = [raw[pl.ds(4 * rc, 4), 4 * g + t].reshape(32, 128) for t in range(4)]
            for lo, part in enumerate(chunk_transpose(parts)):
                a_ref[pl.ds(lo * 128 + rc * 32, 32), pl.ds(g * 128, 128)] = part.astype(BF16)


def right_order_kernel(core_ref, in_ref, keep_ref, send_ref, raw, nat):
    core = core_ref[0]
    raw[...] = in_ref[:, :, 8:16].astype(F32)
    for which, ref in enumerate((keep_ref, send_ref)):
        parity = core if which == 0 else 1 - core
        for g in range(2):
            for qc in range(2):
                parts = [
                    raw[2 * (4 * g + t) + parity, pl.ds(4 * qc, 4)].reshape(32, 128)
                    for t in range(4)
                ]
                for lo, part in enumerate(chunk_transpose(parts)):
                    nat[2 * which + g, pl.ds(qc * 128 + lo, 32, stride=4), :] = part
            ref[:, pl.ds(g * 128, 128)] = nat[2 * which + g].astype(BF16)


def pair_kernel(a_ref, other_ref, keep_ref, send_ref, gate_ref, grad_ref, weight_ref, out_ref, gate_out, grad_out, weight_out, prod):
    weight_out[...] = weight_ref[...]
    gate_out[...] = gate_ref[...]
    grad_out[...] = grad_ref[...]
    value = lax.dot_general(a_ref[...], keep_ref[...], NT, preferred_element_type=F32)
    value += lax.dot_general(other_ref[...], send_ref[...], NT, preferred_element_type=F32)
    for g in range(2):
        prod[g] = value[:, g * 128 : (g + 1) * 128]
    for g in range(2):
        for rc in range(4):
            parts = [prod[g, pl.ds(lo * 128 + rc * 32, 32), :] for lo in range(4)]
            for t, part in enumerate(chunk_transpose(parts)):
                out_ref[pl.ds(4 * rc, 4), 4 * g + t] = part.reshape(4, 8, 128)


def norm_kernel(rounded, pair_ref, gate_ref, grad_ref, weight_ref, gate_out, out_ref, slabs):
    worst = jnp.full((1, 128), -1.0, F32)
    weight = weight_ref[...]
    total = jnp.zeros((128, 128), F32)
    for s in range(8):
        rows = pl.ds(s * 128, 128)
        pair = pair_ref[pl.ds(s, 128, stride=8), :]
        average = jnp.mean(pair, axis=0, keepdims=True)
        centered = pair - average
        variance = jnp.mean(centered * centered, axis=0, keepdims=True)
        inv_std = lax.rsqrt(variance + 1e-05)
        worst = jnp.maximum(worst, average * average + FLOOR - variance)
        normed = centered * inv_std
        normed_half = normed.astype(BF16)
        gate_prob = jax.nn.sigmoid(gate_ref[rows, :].astype(F32))
        upstream = grad_ref[rows, :].astype(F32)
        gated = upstream * gate_prob
        gated_grad = gated.astype(BF16)
        projected = lax.dot_general(normed_half, weight, TN, preferred_element_type=F32)
        gate_out[rows, :] = (gated * projected * (1.0 - gate_prob)).astype(BF16)
        total += jnp.dot(normed_half, gated_grad, preferred_element_type=F32)
        grad_normed = lax.dot_general(weight, gated_grad, NT, preferred_element_type=F32)
        mean_one = jnp.mean(grad_normed, axis=0, keepdims=True)
        mean_two = jnp.mean(grad_normed * normed, axis=0, keepdims=True)
        grad_pair = (grad_normed - mean_one - normed * mean_two) * inv_std
        slabs[pl.ds(s, 128, stride=10), :] = grad_pair
    high, rest = split_halves(total * (1.0 / 512.0))
    if rounded:
        high = jnp.where(jnp.max(worst, axis=1, keepdims=True) > 0.0, jnp.inf, high)
    slabs[pl.ds(8, 128, stride=10), :] = high
    slabs[pl.ds(9, 128, stride=10), :] = rest
    out_ref[...] = slabs[...].astype(BF16)


def half_order(ref, raw, gp):
    raw[...] = ref[...].astype(F32)
    for g in range(2):
        for rc in range(4):
            parts = [
                jnp.concatenate(
                    [raw[pl.ds((8 * r + 4 * g + t) * 10, 8), :] for r in range(4 * rc, 4 * rc + 4)]
                )
                for t in range(4)
            ]
            for lo, part in enumerate(chunk_transpose(parts)):
                gp[pl.ds(lo * 128 + rc * 32, 32), pl.ds(g * 128, 128)] = part.astype(BF16)
    terms = [raw[pl.ds(8 + row, 128, stride=10), :] for row in range(2)]
    return jnp.sum(terms[0], axis=0, keepdims=True) + jnp.sum(terms[1], axis=0, keepdims=True)


def right_kernel(core_ref, own_ref, a_ref, other_ref, gp_ref, sum_ref, out_ref, raw, flat):
    core = core_ref[0]
    sum_ref[...] = jnp.broadcast_to(half_order(own_ref, raw, gp_ref), (8, 128))
    turned = gp_ref[...].T
    for which, ref in enumerate((a_ref, other_ref)):
        parity = core if which == 0 else 1 - core
        value = jnp.dot(turned, ref[...], preferred_element_type=F32)
        for g in range(2):
            flat[2 * which + g] = value[:, g * 128 : (g + 1) * 128]
        for g in range(2):
            for qc in range(2):
                parts = [
                    flat[2 * which + g, pl.ds(qc * 128 + lo, 32, stride=4), :] for lo in range(4)
                ]
                for t, part in enumerate(chunk_transpose(parts)):
                    where = (2 * (4 * g + t) + parity, pl.ds(4 * qc, 4))
                    out_ref[where] = part.reshape(4, 8, 128).astype(BF16)


def left_kernel(far_ref, gp_ref, keep_ref, got_ref, sum_ref, right_ref, out_ref, flag_ref, raw, gp, prod, out):
    total = half_order(far_ref, raw, gp) + sum_ref[0:1, :]
    flag_ref[0] = (jnp.max(total) > 3e38).astype(jnp.int32)
    high, rest = split_halves(total)
    out[pl.ds(16, 128, stride=18), :] = jnp.broadcast_to(high, (128, 128))
    out[pl.ds(17, 128, stride=18), :] = jnp.broadcast_to(rest, (128, 128))
    value = jnp.dot(gp_ref[...], keep_ref[...], preferred_element_type=F32)
    value += jnp.dot(gp[...], got_ref[...], preferred_element_type=F32)
    for g in range(2):
        prod[g] = value[:, g * 128 : (g + 1) * 128]
    for g in range(2):
        for rc in range(4):
            parts = [prod[g, pl.ds(lo * 128 + rc * 32, 32), :] for lo in range(4)]
            for t, part in enumerate(chunk_transpose(parts)):
                for u in range(4):
                    at = (4 * rc + u) * 8 + 4 * g + t
                    out[pl.ds(at * 18, 8), :] = part[8 * u : 8 * u + 8]
                    out[pl.ds(at * 18 + 8, 8), :] = right_ref[4 * rc + u, 4 * g + t].astype(F32)
    out_ref[...] = out[...].astype(BF16)


VM = pl.BlockSpec(memory_space=pltpu.VMEM)
SM = pl.BlockSpec(memory_space=pltpu.SMEM)


def call(kernel, outs, ins, scratch, name, us=1):
    return pl.pallas_call(
        kernel,
        out_shape=[jax.ShapeDtypeStruct(s, d) for s, d in outs],
        in_specs=ins,
        out_specs=[SM if s == (1,) else VM for s, _ in outs],
        scratch_shapes=[pltpu.VMEM(s, d) for s, d in scratch],
        compiler_params=PARAMS,
        cost_estimate=pl.CostEstimate(flops=0, bytes_accessed=3_000_000 * us, transcendentals=0),
        name=name,
    )


def exchange(x):
    return lax.all_to_all(x, ("row", "col"), 0, 0, axis_index_groups=SAME_CORE, tiled=True)


def other_core(x):
    return lax.ppermute(x, "col", [(i, i ^ 1) for i in range(16)])


def local(left_proj, right_proj, gate, out_weight, grad_out):
    core = (lax.axis_index("col") & 1).astype(jnp.int32).reshape(1)
    sides = jnp.concatenate([left_proj.reshape(1024, 128), right_proj.reshape(1024, 128)])
    (packed,) = call(
        pack_kernel, [((128, 16, 128), BF16)], [SM, VM], [((128, 16, 128), F32)], "pack"
    )(core, sides)
    blocks = exchange(packed).reshape(16, 8, 16, 128)
    (a,) = call(
        left_order_kernel, [((512, 256), BF16)], [VM], [((16, 8, 8, 128), F32)], "left_order"
    )(blocks)
    other = other_core(a)
    keep, send = call(
        right_order_kernel,
        [((256, 256), BF16), ((256, 256), BF16)],
        [SM, VM],
        [((16, 8, 8, 128), F32), ((4, 256, 128), F32)],
        "right_order",
    )(core, blocks)
    got = other_core(send)
    other, got = lax.optimization_barrier((other, got))

    def middle(dtype):
        flat = (1024, 128)
        pair, gates, ups, weight = call(
            pair_kernel,
            [((16, 8, 8, 128), F32), (flat, BF16), (flat, BF16), ((128, 128), BF16)],
            [VM] * 7,
            [((2, 512, 128), F32)],
            "pair",
        )(a, other, keep, send, gate.reshape(flat), grad_out.reshape(flat), out_weight)
        pair = exchange(pair.reshape(128, 8, 128).astype(dtype)).astype(F32)
        grad_gate, grad_pair = call(
            functools.partial(norm_kernel, dtype != F32),
            [((1024, 128), BF16), ((1280, 128), BF16)],
            [VM] * 4,
            [((1280, 128), F32)],
            "norm",
        )(pair.reshape(flat), gates, ups, weight)
        own = exchange(grad_pair.reshape(128, 5, 2, 128))
        far = other_core(own)
        half, total, right = call(
            right_kernel,
            [((512, 256), BF16), ((8, 128), F32), ((16, 8, 8, 128), BF16)],
            [SM] + [VM] * 3,
            [((1280, 128), F32), ((4, 256, 128), F32)],
            "right",
        )(core, own.reshape(1280, 128), a, other)
        grads, flag = call(
            left_kernel,
            [((2304, 128), BF16), ((1,), jnp.int32)],
            [VM] * 6,
            [((1280, 128), F32), ((512, 256), BF16), ((2, 512, 128), F32), ((2304, 128), F32)],
            "left",
        )(far.reshape(1280, 128), half, keep, got, total, right)
        grads = exchange(grads.reshape(128, 9, 2, 128))
        grad_left, grad_right, grad_weight = call(
            unpack_kernel,
            [((1024, 128), BF16), ((1024, 128), BF16), ((128, 128), F32)],
            [VM],
            [((2304, 128), F32)],
            "unpack",
        )(grads.reshape(2304, 128))
        return flag[0], (grad_left, grad_right, grad_gate, grad_weight)

    flag, outs = middle(jnp.float16)
    left, right, gates, weight = lax.cond(flag > 0, lambda: middle(F32)[1], lambda: outs)
    shape = (32, 32, 128)
    return left.reshape(shape), right.reshape(shape), gates.reshape(shape), weight


def solution(mesh):
    return jax.shard_map(
        local,
        mesh=mesh,
        in_specs=(
            P("row", "col", None),
            P("col", "row", None),
            P("row", "col", None),
            P(),
            P("row", "col", None),
        ),
        out_specs=(P("row", "col", None), P("col", "row", None), P("row", "col", None), P()),
        check_vma=False,
    )
```

```python
import functools

import jax
import jax.numpy as jnp
from jax import lax
from jax.experimental import pallas as pl
from jax.experimental.pallas import tpu as pltpu
from jax.sharding import PartitionSpec as P

F32 = jnp.float32
BF16 = jnp.bfloat16
PARAMS = pltpu.CompilerParams(vmem_limit_bytes=32 * 1024 * 1024)
NT = (((1,), (1,)), ((), ()))
TN = (((0,), (0,)), ((), ()))
FLOOR = 1e-07

SAME_CORE = [[row * 16 + col for row in range(16) for col in range(core, 16, 2)] for core in (0, 1)]


def chunk_transpose(parts):
    lane = lax.broadcasted_iota(jnp.int32, parts[0].shape, 1)
    low = lane < 64
    even = (lane & 32) == 0
    turn = lambda x, by: pltpu.roll(x, by, 1)
    y0, y1, y2, y3 = parts
    a0 = jnp.where(low, y0, turn(y2, 64))
    a2 = jnp.where(low, turn(y0, 64), y2)
    a1 = jnp.where(low, y1, turn(y3, 64))
    a3 = jnp.where(low, turn(y1, 64), y3)
    return [
        jnp.where(even, a0, turn(a1, 32)),
        jnp.where(even, turn(a0, 96), a1),
        jnp.where(even, a2, turn(a3, 32)),
        jnp.where(even, turn(a2, 96), a3),
    ]


def split_halves(x):
    high = x.astype(BF16).astype(F32)
    return high, (x - high).astype(BF16).astype(F32)


def pack_kernel(core_ref, in_ref, out_ref, slabs):
    for side in range(2):
        for s in range(8):
            slab = in_ref[pl.ds(side * 1024 + s * 128, 128), :].astype(F32)
            slabs[:, side * 8 + s, :] = slab.T
    out_ref[...] = slabs[...].astype(BF16)


def unpack_kernel(in_ref, left_ref, right_ref, weight_ref, slabs):
    slabs[...] = in_ref[...].astype(F32)
    for side, ref in enumerate((left_ref, right_ref)):
        for s in range(8):
            slab = slabs[pl.ds(side * 8 + s, 128, stride=18), :]
            ref[pl.ds(s * 128, 128), :] = slab.T.astype(BF16)
    weight_ref[...] = slabs[pl.ds(16, 128, stride=18), :] + slabs[pl.ds(17, 128, stride=18), :]


def left_order_kernel(in_ref, a_ref, raw):
    raw[...] = in_ref[:, :, 0:8].astype(F32)
    for g in range(2):
        for rc in range(4):
            parts = [raw[pl.ds(4 * rc, 4), 4 * g + t].reshape(32, 128) for t in range(4)]
            for lo, part in enumerate(chunk_transpose(parts)):
                a_ref[pl.ds(lo * 128 + rc * 32, 32), pl.ds(g * 128, 128)] = part.astype(BF16)


def right_order_kernel(core_ref, in_ref, keep_ref, send_ref, raw, nat):
    core = core_ref[0]
    raw[...] = in_ref[:, :, 8:16].astype(F32)
    for which, ref in enumerate((keep_ref, send_ref)):
        parity = core if which == 0 else 1 - core
        for g in range(2):
            for qc in range(2):
                parts = [
                    raw[2 * (4 * g + t) + parity, pl.ds(4 * qc, 4)].reshape(32, 128)
                    for t in range(4)
                ]
                for lo, part in enumerate(chunk_transpose(parts)):
                    nat[2 * which + g, pl.ds(qc * 128 + lo, 32, stride=4), :] = part
            ref[:, pl.ds(g * 128, 128)] = nat[2 * which + g].astype(BF16)


def pair_kernel(a_ref, other_ref, keep_ref, send_ref, gate_ref, grad_ref, weight_ref, out_ref, gate_out, grad_out, weight_out, prod):
    weight_out[...] = weight_ref[...]
    gate_out[...] = gate_ref[...]
    grad_out[...] = grad_ref[...]
    value = lax.dot_general(a_ref[...], keep_ref[...], NT, preferred_element_type=F32)
    value += lax.dot_general(other_ref[...], send_ref[...], NT, preferred_element_type=F32)
    for g in range(2):
        prod[g] = value[:, g * 128 : (g + 1) * 128]
    for g in range(2):
        for rc in range(4):
            parts = [prod[g, pl.ds(lo * 128 + rc * 32, 32), :] for lo in range(4)]
            for t, part in enumerate(chunk_transpose(parts)):
                out_ref[pl.ds(4 * rc, 4), 4 * g + t] = part.reshape(4, 8, 128)


def norm_kernel(rounded, pair_ref, gate_ref, grad_ref, weight_ref, gate_out, out_ref, slabs):
    worst = jnp.full((1, 128), -1.0, F32)
    weight = weight_ref[...]
    total = jnp.zeros((128, 128), F32)
    for s in range(8):
        rows = pl.ds(s * 128, 128)
        pair = pair_ref[pl.ds(s, 128, stride=8), :]
        average = jnp.mean(pair, axis=0, keepdims=True)
        centered = pair - average
        variance = jnp.mean(centered * centered, axis=0, keepdims=True)
        inv_std = lax.rsqrt(variance + 1e-05)
        worst = jnp.maximum(worst, average * average + FLOOR - variance)
        normed = centered * inv_std
        normed_half = normed.astype(BF16)
        gate_prob = jax.nn.sigmoid(gate_ref[rows, :].astype(F32))
        upstream = grad_ref[rows, :].astype(F32)
        gated = upstream * gate_prob
        gated_grad = gated.astype(BF16)
        projected = lax.dot_general(normed_half, weight, TN, preferred_element_type=F32)
        gate_out[rows, :] = (gated * projected * (1.0 - gate_prob)).astype(BF16)
        total += jnp.dot(normed_half, gated_grad, preferred_element_type=F32)
        grad_normed = lax.dot_general(weight, gated_grad, NT, preferred_element_type=F32)
        mean_one = jnp.mean(grad_normed, axis=0, keepdims=True)
        mean_two = jnp.mean(grad_normed * normed, axis=0, keepdims=True)
        grad_pair = (grad_normed - mean_one - normed * mean_two) * inv_std
        slabs[pl.ds(s, 128, stride=10), :] = grad_pair
    high, rest = split_halves(total * (1.0 / 512.0))
    if rounded:
        high = jnp.where(jnp.max(worst, axis=1, keepdims=True) > 0.0, jnp.inf, high)
    slabs[pl.ds(8, 128, stride=10), :] = high
    slabs[pl.ds(9, 128, stride=10), :] = rest
    out_ref[...] = slabs[...].astype(BF16)


def half_order(ref, raw, gp):
    raw[...] = ref[...].astype(F32)
    for g in range(2):
        for rc in range(4):
            parts = [
                jnp.concatenate(
                    [raw[pl.ds((8 * r + 4 * g + t) * 10, 8), :] for r in range(4 * rc, 4 * rc + 4)]
                )
                for t in range(4)
            ]
            for lo, part in enumerate(chunk_transpose(parts)):
                gp[pl.ds(lo * 128 + rc * 32, 32), pl.ds(g * 128, 128)] = part.astype(BF16)
    terms = [raw[pl.ds(8 + row, 128, stride=10), :] for row in range(2)]
    return jnp.sum(terms[0], axis=0, keepdims=True) + jnp.sum(terms[1], axis=0, keepdims=True)


def right_kernel(core_ref, own_ref, a_ref, other_ref, gp_ref, sum_ref, out_ref, raw, flat):
    core = core_ref[0]
    sum_ref[...] = jnp.broadcast_to(half_order(own_ref, raw, gp_ref), (8, 128))
    turned = gp_ref[...].T
    for which, ref in enumerate((a_ref, other_ref)):
        parity = core if which == 0 else 1 - core
        value = jnp.dot(turned, ref[...], preferred_element_type=F32)
        for g in range(2):
            flat[2 * which + g] = value[:, g * 128 : (g + 1) * 128]
        for g in range(2):
            for qc in range(2):
                parts = [
                    flat[2 * which + g, pl.ds(qc * 128 + lo, 32, stride=4), :] for lo in range(4)
                ]
                for t, part in enumerate(chunk_transpose(parts)):
                    where = (2 * (4 * g + t) + parity, pl.ds(4 * qc, 4))
                    out_ref[where] = part.reshape(4, 8, 128).astype(BF16)


def left_kernel(far_ref, gp_ref, keep_ref, got_ref, sum_ref, right_ref, out_ref, flag_ref, raw, gp, prod, out):
    total = half_order(far_ref, raw, gp) + sum_ref[0:1, :]
    flag_ref[0] = (jnp.max(total) > 3e38).astype(jnp.int32)
    high, rest = split_halves(total)
    out[pl.ds(16, 128, stride=18), :] = jnp.broadcast_to(high, (128, 128))
    out[pl.ds(17, 128, stride=18), :] = jnp.broadcast_to(rest, (128, 128))
    value = jnp.dot(gp_ref[...], keep_ref[...], preferred_element_type=F32)
    value += jnp.dot(gp[...], got_ref[...], preferred_element_type=F32)
    for g in range(2):
        prod[g] = value[:, g * 128 : (g + 1) * 128]
    for g in range(2):
        for rc in range(4):
            parts = [prod[g, pl.ds(lo * 128 + rc * 32, 32), :] for lo in range(4)]
            for t, part in enumerate(chunk_transpose(parts)):
                for u in range(4):
                    at = (4 * rc + u) * 8 + 4 * g + t
                    out[pl.ds(at * 18, 8), :] = part[8 * u : 8 * u + 8]
                    out[pl.ds(at * 18 + 8, 8), :] = right_ref[4 * rc + u, 4 * g + t].astype(F32)
    out_ref[...] = out[...].astype(BF16)


VM = pl.BlockSpec(memory_space=pltpu.VMEM)
SM = pl.BlockSpec(memory_space=pltpu.SMEM)


def call(kernel, outs, ins, scratch, name, us=1):
    return pl.pallas_call(
        kernel,
        out_shape=[jax.ShapeDtypeStruct(s, d) for s, d in outs],
        in_specs=ins,
        out_specs=[SM if s == (1,) else VM for s, _ in outs],
        scratch_shapes=[pltpu.VMEM(s, d) for s, d in scratch],
        compiler_params=PARAMS,
        cost_estimate=pl.CostEstimate(flops=0, bytes_accessed=3_000_000 * us, transcendentals=0),
        name=name,
    )


def exchange(x):
    return lax.all_to_all(x, ("row", "col"), 0, 0, axis_index_groups=SAME_CORE, tiled=True)


def other_core(x):
    return lax.ppermute(x, "col", [(i, i ^ 1) for i in range(16)])


def local(left_proj, right_proj, gate, out_weight, grad_out):
    core = (lax.axis_index("col") & 1).astype(jnp.int32).reshape(1)
    sides = jnp.concatenate([left_proj.reshape(1024, 128), right_proj.reshape(1024, 128)])
    (packed,) = call(
        pack_kernel, [((128, 16, 128), BF16)], [SM, VM], [((128, 16, 128), F32)], "pack"
    )(core, sides)
    blocks = exchange(packed).reshape(16, 8, 16, 128)
    (a,) = call(
        left_order_kernel, [((512, 256), BF16)], [VM], [((16, 8, 8, 128), F32)], "left_order"
    )(blocks)
    other = other_core(a)
    keep, send = call(
        right_order_kernel,
        [((256, 256), BF16), ((256, 256), BF16)],
        [SM, VM],
        [((16, 8, 8, 128), F32), ((4, 256, 128), F32)],
        "right_order",
    )(core, blocks)

    def middle(dtype):
        flat = (1024, 128)
        pair, gates, ups, weight = call(
            pair_kernel,
            [((16, 8, 8, 128), F32), (flat, BF16), (flat, BF16), ((128, 128), BF16)],
            [VM] * 7,
            [((2, 512, 128), F32)],
            "pair",
        )(a, other, keep, send, gate.reshape(flat), grad_out.reshape(flat), out_weight)
        pair = exchange(pair.reshape(128, 8, 128).astype(dtype)).astype(F32)
        grad_gate, grad_pair = call(
            functools.partial(norm_kernel, dtype != F32),
            [((1024, 128), BF16), ((1280, 128), BF16)],
            [VM] * 4,
            [((1280, 128), F32)],
            "norm",
        )(pair.reshape(flat), gates, ups, weight)
        own = exchange(grad_pair.reshape(128, 5, 2, 128))
        far = other_core(own)
        got = other_core(send)
        half, total, right = call(
            right_kernel,
            [((512, 256), BF16), ((8, 128), F32), ((16, 8, 8, 128), BF16)],
            [SM] + [VM] * 3,
            [((1280, 128), F32), ((4, 256, 128), F32)],
            "right",
        )(core, own.reshape(1280, 128), a, other)
        grads, flag = call(
            left_kernel,
            [((2304, 128), BF16), ((1,), jnp.int32)],
            [VM] * 6,
            [((1280, 128), F32), ((512, 256), BF16), ((2, 512, 128), F32), ((2304, 128), F32)],
            "left",
        )(far.reshape(1280, 128), half, keep, got, total, right)
        grads = exchange(grads.reshape(128, 9, 2, 128))
        grad_left, grad_right, grad_weight = call(
            unpack_kernel,
            [((1024, 128), BF16), ((1024, 128), BF16), ((128, 128), F32)],
            [VM],
            [((2304, 128), F32)],
            "unpack",
        )(grads.reshape(2304, 128))
        return flag[0], (grad_left, grad_right, grad_gate, grad_weight)

    flag, outs = middle(jnp.float16)
    left, right, gates, weight = lax.cond(flag > 0, lambda: middle(F32)[1], lambda: outs)
    shape = (32, 32, 128)
    return left.reshape(shape), right.reshape(shape), gates.reshape(shape), weight


def solution(mesh):
    return jax.shard_map(
        local,
        mesh=mesh,
        in_specs=(
            P("row", "col", None),
            P("col", "row", None),
            P("row", "col", None),
            P(),
            P("row", "col", None),
        ),
        out_specs=(P("row", "col", None), P("col", "row", None), P("row", "col", None), P()),
        check_vma=False,
    )
```

```python
import functools

import jax
import jax.numpy as jnp
from jax import lax
from jax.experimental import pallas as pl
from jax.experimental.pallas import tpu as pltpu
from jax.sharding import PartitionSpec as P

F32 = jnp.float32
BF16 = jnp.bfloat16
PARAMS = pltpu.CompilerParams(vmem_limit_bytes=32 * 1024 * 1024)
NT = (((1,), (1,)), ((), ()))
TN = (((0,), (0,)), ((), ()))
FLOOR = 1e-07

SAME_CORE = [[row * 16 + col for row in range(16) for col in range(core, 16, 2)] for core in (0, 1)]


def chunk_transpose(parts):
    lane = lax.broadcasted_iota(jnp.int32, parts[0].shape, 1)
    low = lane < 64
    even = (lane & 32) == 0
    turn = lambda x, by: pltpu.roll(x, by, 1)
    y0, y1, y2, y3 = parts
    a0 = jnp.where(low, y0, turn(y2, 64))
    a2 = jnp.where(low, turn(y0, 64), y2)
    a1 = jnp.where(low, y1, turn(y3, 64))
    a3 = jnp.where(low, turn(y1, 64), y3)
    return [
        jnp.where(even, a0, turn(a1, 32)),
        jnp.where(even, turn(a0, 96), a1),
        jnp.where(even, a2, turn(a3, 32)),
        jnp.where(even, turn(a2, 96), a3),
    ]


def split_halves(x):
    high = x.astype(BF16).astype(F32)
    return high, (x - high).astype(BF16).astype(F32)


def pack_kernel(core_ref, in_ref, out_ref, slabs):
    for side in range(2):
        for s in range(8):
            slab = in_ref[pl.ds(side * 1024 + s * 128, 128), :].astype(F32)
            slabs[:, side * 8 + s, :] = slab.T
    out_ref[...] = slabs[...].astype(BF16)


def unpack_kernel(in_ref, left_ref, right_ref, weight_ref, slabs):
    slabs[...] = in_ref[...].astype(F32)
    for side, ref in enumerate((left_ref, right_ref)):
        for s in range(8):
            slab = slabs[pl.ds(side * 8 + s, 128, stride=18), :]
            ref[pl.ds(s * 128, 128), :] = slab.T.astype(BF16)
    weight_ref[...] = slabs[pl.ds(16, 128, stride=18), :] + slabs[pl.ds(17, 128, stride=18), :]


def left_order_kernel(in_ref, a_ref, raw):
    raw[...] = in_ref[:, :, 0:8].astype(F32)
    for g in range(2):
        for rc in range(4):
            parts = [raw[pl.ds(4 * rc, 4), 4 * g + t].reshape(32, 128) for t in range(4)]
            for lo, part in enumerate(chunk_transpose(parts)):
                a_ref[pl.ds(lo * 128 + rc * 32, 32), pl.ds(g * 128, 128)] = part.astype(BF16)


def right_order_kernel(core_ref, in_ref, keep_ref, send_ref, raw, nat):
    core = core_ref[0]
    raw[...] = in_ref[:, :, 8:16].astype(F32)
    for which, ref in enumerate((keep_ref, send_ref)):
        parity = core if which == 0 else 1 - core
        for g in range(2):
            for qc in range(2):
                parts = [
                    raw[2 * (4 * g + t) + parity, pl.ds(4 * qc, 4)].reshape(32, 128)
                    for t in range(4)
                ]
                for lo, part in enumerate(chunk_transpose(parts)):
                    nat[2 * which + g, pl.ds(qc * 128 + lo, 32, stride=4), :] = part
            ref[:, pl.ds(g * 128, 128)] = nat[2 * which + g].astype(BF16)


def pair_kernel(a_ref, other_ref, keep_ref, send_ref, gate_ref, grad_ref, weight_ref, out_ref, gate_out, grad_out, weight_out, prod):
    weight_out[...] = weight_ref[...]
    gate_out[...] = gate_ref[...]
    grad_out[...] = grad_ref[...]
    value = lax.dot_general(a_ref[...], keep_ref[...], NT, preferred_element_type=F32)
    value += lax.dot_general(other_ref[...], send_ref[...], NT, preferred_element_type=F32)
    for g in range(2):
        prod[g] = value[:, g * 128 : (g + 1) * 128]
    for g in range(2):
        for rc in range(4):
            parts = [prod[g, pl.ds(lo * 128 + rc * 32, 32), :] for lo in range(4)]
            for t, part in enumerate(chunk_transpose(parts)):
                out_ref[pl.ds(4 * rc, 4), 4 * g + t] = part.reshape(4, 8, 128)


def norm_kernel(rounded, pair_ref, gate_ref, grad_ref, weight_ref, gate_out, out_ref, slabs):
    worst = jnp.full((1, 128), -1.0, F32)
    weight = weight_ref[...]
    total = jnp.zeros((128, 128), F32)
    for s in range(8):
        rows = pl.ds(s * 128, 128)
        pair = pair_ref[pl.ds(s, 128, stride=8), :]
        average = jnp.mean(pair, axis=0, keepdims=True)
        centered = pair - average
        variance = jnp.mean(centered * centered, axis=0, keepdims=True)
        inv_std = lax.rsqrt(variance + 1e-05)
        worst = jnp.maximum(worst, average * average + FLOOR - variance)
        normed = centered * inv_std
        normed_half = normed.astype(BF16)
        gate_prob = jax.nn.sigmoid(gate_ref[rows, :].astype(F32))
        upstream = grad_ref[rows, :].astype(F32)
        gated = upstream * gate_prob
        gated_grad = gated.astype(BF16)
        projected = lax.dot_general(normed_half, weight, TN, preferred_element_type=F32)
        gate_out[rows, :] = (gated * projected * (1.0 - gate_prob)).astype(BF16)
        total += jnp.dot(normed_half, gated_grad, preferred_element_type=F32)
        grad_normed = lax.dot_general(weight, gated_grad, NT, preferred_element_type=F32)
        mean_one = jnp.mean(grad_normed, axis=0, keepdims=True)
        mean_two = jnp.mean(grad_normed * normed, axis=0, keepdims=True)
        grad_pair = (grad_normed - mean_one - normed * mean_two) * inv_std
        slabs[pl.ds(s, 128, stride=10), :] = grad_pair
    high, rest = split_halves(total * (1.0 / 512.0))
    if rounded:
        high = jnp.where(jnp.max(worst, axis=1, keepdims=True) > 0.0, jnp.inf, high)
    slabs[pl.ds(8, 128, stride=10), :] = high
    slabs[pl.ds(9, 128, stride=10), :] = rest
    out_ref[...] = slabs[...].astype(BF16)


def half_order(ref, raw, gp):
    raw[...] = ref[...].astype(F32)
    for g in range(2):
        for rc in range(4):
            parts = [
                jnp.concatenate(
                    [raw[pl.ds((8 * r + 4 * g + t) * 10, 8), :] for r in range(4 * rc, 4 * rc + 4)]
                )
                for t in range(4)
            ]
            for lo, part in enumerate(chunk_transpose(parts)):
                gp[pl.ds(lo * 128 + rc * 32, 32), pl.ds(g * 128, 128)] = part.astype(BF16)
    terms = [raw[pl.ds(8 + row, 128, stride=10), :] for row in range(2)]
    return jnp.sum(terms[0], axis=0, keepdims=True) + jnp.sum(terms[1], axis=0, keepdims=True)


def right_kernel(core_ref, own_ref, a_ref, other_ref, gate_ref, gp_ref, sum_ref, out_ref, raw, flat):
    core = core_ref[0]
    sum_ref[...] = jnp.broadcast_to(half_order(own_ref, raw, gp_ref), (8, 128))
    turned = gp_ref[...].T
    for which, ref in enumerate((a_ref, other_ref)):
        parity = core if which == 0 else 1 - core
        value = jnp.dot(turned, ref[...], preferred_element_type=F32)
        for g in range(2):
            flat[2 * which + g] = value[:, g * 128 : (g + 1) * 128]
        for g in range(2):
            for qc in range(2):
                parts = [
                    flat[2 * which + g, pl.ds(qc * 128 + lo, 32, stride=4), :] for lo in range(4)
                ]
                for t, part in enumerate(chunk_transpose(parts)):
                    where = (2 * (4 * g + t) + parity, pl.ds(4 * qc, 4))
                    out_ref[where] = part.reshape(4, 8, 128).astype(BF16)


def left_kernel(far_ref, gp_ref, keep_ref, got_ref, sum_ref, right_ref, out_ref, flag_ref, raw, gp, prod, out):
    total = half_order(far_ref, raw, gp) + sum_ref[0:1, :]
    flag_ref[0] = (jnp.max(total) > 3e38).astype(jnp.int32)
    high, rest = split_halves(total)
    out[pl.ds(16, 128, stride=18), :] = jnp.broadcast_to(high, (128, 128))
    out[pl.ds(17, 128, stride=18), :] = jnp.broadcast_to(rest, (128, 128))
    value = jnp.dot(gp_ref[...], keep_ref[...], preferred_element_type=F32)
    value += jnp.dot(gp[...], got_ref[...], preferred_element_type=F32)
    for g in range(2):
        prod[g] = value[:, g * 128 : (g + 1) * 128]
    for g in range(2):
        for rc in range(4):
            parts = [prod[g, pl.ds(lo * 128 + rc * 32, 32), :] for lo in range(4)]
            for t, part in enumerate(chunk_transpose(parts)):
                for u in range(4):
                    at = (4 * rc + u) * 8 + 4 * g + t
                    out[pl.ds(at * 18, 8), :] = part[8 * u : 8 * u + 8]
                    out[pl.ds(at * 18 + 8, 8), :] = right_ref[4 * rc + u, 4 * g + t].astype(F32)
    out_ref[...] = out[...].astype(BF16)


VM = pl.BlockSpec(memory_space=pltpu.VMEM)
SM = pl.BlockSpec(memory_space=pltpu.SMEM)


def call(kernel, outs, ins, scratch, name, us=1):
    return pl.pallas_call(
        kernel,
        out_shape=[jax.ShapeDtypeStruct(s, d) for s, d in outs],
        in_specs=ins,
        out_specs=[SM if s == (1,) else VM for s, _ in outs],
        scratch_shapes=[pltpu.VMEM(s, d) for s, d in scratch],
        compiler_params=PARAMS,
        cost_estimate=pl.CostEstimate(flops=0, bytes_accessed=3_000_000 * us, transcendentals=0),
        name=name,
    )


def exchange(x):
    return lax.all_to_all(x, ("row", "col"), 0, 0, axis_index_groups=SAME_CORE, tiled=True)


def other_core(x):
    return lax.ppermute(x, "col", [(i, i ^ 1) for i in range(16)])


def local(left_proj, right_proj, gate, out_weight, grad_out):
    core = (lax.axis_index("col") & 1).astype(jnp.int32).reshape(1)
    sides = jnp.concatenate([left_proj.reshape(1024, 128), right_proj.reshape(1024, 128)])
    (packed,) = call(
        pack_kernel, [((128, 16, 128), BF16)], [SM, VM], [((128, 16, 128), F32)], "pack"
    )(core, sides)
    blocks = exchange(packed).reshape(16, 8, 16, 128)
    (a,) = call(
        left_order_kernel, [((512, 256), BF16)], [VM], [((16, 8, 8, 128), F32)], "left_order"
    )(blocks)
    other = other_core(a)
    keep, send = call(
        right_order_kernel,
        [((256, 256), BF16), ((256, 256), BF16)],
        [SM, VM],
        [((16, 8, 8, 128), F32), ((4, 256, 128), F32)],
        "right_order",
    )(core, blocks)

    def middle(dtype):
        flat = (1024, 128)
        pair, gates, ups, weight = call(
            pair_kernel,
            [((16, 8, 8, 128), F32), (flat, BF16), (flat, BF16), ((128, 128), BF16)],
            [VM] * 7,
            [((2, 512, 128), F32)],
            "pair",
        )(a, other, keep, send, gate.reshape(flat), grad_out.reshape(flat), out_weight)
        pair = exchange(pair.reshape(128, 8, 128).astype(dtype)).astype(F32)
        grad_gate, grad_pair = call(
            functools.partial(norm_kernel, dtype != F32),
            [((1024, 128), BF16), ((1280, 128), BF16)],
            [VM] * 4,
            [((1280, 128), F32)],
            "norm",
        )(pair.reshape(flat), gates, ups, weight)
        own = exchange(grad_pair.reshape(128, 5, 2, 128))
        far = other_core(own)
        got = other_core(send)
        half, total, right = call(
            right_kernel,
            [((512, 256), BF16), ((8, 128), F32), ((16, 8, 8, 128), BF16)],
            [SM] + [VM] * 4,
            [((1280, 128), F32), ((4, 256, 128), F32)],
            "right",
        )(core, own.reshape(1280, 128), a, other, grad_gate)
        grads, flag = call(
            left_kernel,
            [((2304, 128), BF16), ((1,), jnp.int32)],
            [VM] * 6,
            [((1280, 128), F32), ((512, 256), BF16), ((2, 512, 128), F32), ((2304, 128), F32)],
            "left",
        )(far.reshape(1280, 128), half, keep, got, total, right)
        grads = exchange(grads.reshape(128, 9, 2, 128))
        grad_left, grad_right, grad_weight = call(
            unpack_kernel,
            [((1024, 128), BF16), ((1024, 128), BF16), ((128, 128), F32)],
            [VM],
            [((2304, 128), F32)],
            "unpack",
        )(grads.reshape(2304, 128))
        return flag[0], (grad_left, grad_right, grad_gate, grad_weight)

    flag, outs = middle(jnp.float16)
    left, right, gates, weight = lax.cond(flag > 0, lambda: middle(F32)[1], lambda: outs)
    shape = (32, 32, 128)
    return left.reshape(shape), right.reshape(shape), gates.reshape(shape), weight


def solution(mesh):
    return jax.shard_map(
        local,
        mesh=mesh,
        in_specs=(
            P("row", "col", None),
            P("col", "row", None),
            P("row", "col", None),
            P(),
            P("row", "col", None),
        ),
        out_specs=(P("row", "col", None), P("col", "row", None), P("row", "col", None), P()),
        check_vma=False,
    )
```

```python
import functools

import jax
import jax.numpy as jnp
from jax import lax
from jax.experimental import pallas as pl
from jax.experimental.pallas import tpu as pltpu
from jax.sharding import PartitionSpec as P

F32 = jnp.float32
BF16 = jnp.bfloat16
PARAMS = pltpu.CompilerParams(vmem_limit_bytes=32 * 1024 * 1024)
NT = (((1,), (1,)), ((), ()))
TN = (((0,), (0,)), ((), ()))
FLOOR = 1e-07

SAME_CORE = [[row * 16 + col for row in range(16) for col in range(core, 16, 2)] for core in (0, 1)]


def chunk_transpose(parts):
    lane = lax.broadcasted_iota(jnp.int32, parts[0].shape, 1)
    low = lane < 64
    even = (lane & 32) == 0
    turn = lambda x, by: pltpu.roll(x, by, 1)
    y0, y1, y2, y3 = parts
    a0 = jnp.where(low, y0, turn(y2, 64))
    a2 = jnp.where(low, turn(y0, 64), y2)
    a1 = jnp.where(low, y1, turn(y3, 64))
    a3 = jnp.where(low, turn(y1, 64), y3)
    return [
        jnp.where(even, a0, turn(a1, 32)),
        jnp.where(even, turn(a0, 96), a1),
        jnp.where(even, a2, turn(a3, 32)),
        jnp.where(even, turn(a2, 96), a3),
    ]


def split_halves(x):
    high = x.astype(BF16).astype(F32)
    return high, (x - high).astype(BF16).astype(F32)


def pack_kernel(core_ref, in_ref, out_ref, slabs):
    for side in range(2):
        for s in range(8):
            slab = in_ref[pl.ds(side * 1024 + s * 128, 128), :].astype(F32)
            slabs[:, side * 8 + s, :] = slab.T
    out_ref[...] = slabs[...].astype(BF16)


def unpack_kernel(in_ref, left_ref, right_ref, weight_ref, slabs):
    slabs[...] = in_ref[...].astype(F32)
    for side, ref in enumerate((left_ref, right_ref)):
        for s in range(8):
            slab = slabs[pl.ds(side * 8 + s, 128, stride=18), :]
            ref[pl.ds(s * 128, 128), :] = slab.T.astype(BF16)
    weight_ref[...] = slabs[pl.ds(16, 128, stride=18), :] + slabs[pl.ds(17, 128, stride=18), :]


def left_order_kernel(in_ref, a_ref, raw):
    raw[...] = in_ref[:, :, 0:8].astype(F32)
    for g in range(2):
        for rc in range(4):
            parts = [raw[pl.ds(4 * rc, 4), 4 * g + t].reshape(32, 128) for t in range(4)]
            for lo, part in enumerate(chunk_transpose(parts)):
                a_ref[pl.ds(lo * 128 + rc * 32, 32), pl.ds(g * 128, 128)] = part.astype(BF16)


def right_order_kernel(core_ref, in_ref, keep_ref, send_ref, raw, nat):
    core = core_ref[0]
    raw[...] = in_ref[:, :, 8:16].astype(F32)
    for which, ref in enumerate((keep_ref, send_ref)):
        parity = core if which == 0 else 1 - core
        for g in range(2):
            for qc in range(2):
                parts = [
                    raw[2 * (4 * g + t) + parity, pl.ds(4 * qc, 4)].reshape(32, 128)
                    for t in range(4)
                ]
                for lo, part in enumerate(chunk_transpose(parts)):
                    nat[2 * which + g, pl.ds(qc * 128 + lo, 32, stride=4), :] = part
            ref[:, pl.ds(g * 128, 128)] = nat[2 * which + g].astype(BF16)


def pair_kernel(a_ref, other_ref, keep_ref, send_ref, gate_ref, grad_ref, weight_ref, out_ref, gate_out, grad_out, weight_out, prod):
    weight_out[...] = weight_ref[...]
    gate_out[...] = gate_ref[...]
    grad_out[...] = grad_ref[...]
    value = lax.dot_general(a_ref[...], keep_ref[...], NT, preferred_element_type=F32)
    value += lax.dot_general(other_ref[...], send_ref[...], NT, preferred_element_type=F32)
    for g in range(2):
        prod[g] = value[:, g * 128 : (g + 1) * 128]
    for g in range(2):
        for rc in range(4):
            parts = [prod[g, pl.ds(lo * 128 + rc * 32, 32), :] for lo in range(4)]
            for t, part in enumerate(chunk_transpose(parts)):
                out_ref[pl.ds(4 * rc, 4), 4 * g + t] = part.reshape(4, 8, 128)


def norm_kernel(rounded, pair_ref, gate_ref, grad_ref, weight_ref, gate_out, out_ref, slabs):
    worst = jnp.full((1, 128), -1.0, F32)
    weight = weight_ref[...]
    total = jnp.zeros((128, 128), F32)
    for s in range(8):
        rows = pl.ds(s * 128, 128)
        pair = pair_ref[pl.ds(s, 128, stride=8), :]
        average = jnp.mean(pair, axis=0, keepdims=True)
        centered = pair - average
        variance = jnp.mean(centered * centered, axis=0, keepdims=True)
        inv_std = lax.rsqrt(variance + 1e-05)
        worst = jnp.maximum(worst, average * average + FLOOR - variance)
        normed = centered * inv_std
        normed_half = normed.astype(BF16)
        gate_prob = jax.nn.sigmoid(gate_ref[rows, :].astype(F32))
        upstream = grad_ref[rows, :].astype(F32)
        gated = upstream * gate_prob
        gated_grad = gated.astype(BF16)
        projected = lax.dot_general(normed_half, weight, TN, preferred_element_type=F32)
        gate_out[rows, :] = (gated * projected * (1.0 - gate_prob)).astype(BF16)
        total += jnp.dot(normed_half, gated_grad, preferred_element_type=F32)
        grad_normed = lax.dot_general(weight, gated_grad, NT, preferred_element_type=F32)
        mean_one = jnp.mean(grad_normed, axis=0, keepdims=True)
        mean_two = jnp.mean(grad_normed * normed, axis=0, keepdims=True)
        grad_pair = (grad_normed - mean_one - normed * mean_two) * inv_std
        slabs[pl.ds(s, 128, stride=10), :] = grad_pair
    high, rest = split_halves(total * (1.0 / 512.0))
    if rounded:
        high = jnp.where(jnp.max(worst, axis=1, keepdims=True) > 0.0, jnp.inf, high)
    slabs[pl.ds(8, 128, stride=10), :] = high
    slabs[pl.ds(9, 128, stride=10), :] = rest
    out_ref[...] = slabs[...].astype(BF16)


def half_order(ref, raw, gp):
    raw[...] = ref[...].astype(F32)
    for g in range(2):
        for rc in range(4):
            parts = [
                jnp.concatenate(
                    [raw[pl.ds((8 * r + 4 * g + t) * 10, 8), :] for r in range(4 * rc, 4 * rc + 4)]
                )
                for t in range(4)
            ]
            for lo, part in enumerate(chunk_transpose(parts)):
                gp[pl.ds(lo * 128 + rc * 32, 32), pl.ds(g * 128, 128)] = part.astype(BF16)
    terms = [raw[pl.ds(8 + row, 128, stride=10), :] for row in range(2)]
    return jnp.sum(terms[0], axis=0, keepdims=True) + jnp.sum(terms[1], axis=0, keepdims=True)


def right_kernel(core_ref, own_ref, a_ref, other_ref, gate_ref, gp_ref, sum_ref, out_ref, raw, flat):
    core = core_ref[0]
    sum_ref[...] = jnp.broadcast_to(half_order(own_ref, raw, gp_ref), (8, 128))
    turned = gp_ref[...].T
    for which, ref in enumerate((a_ref, other_ref)):
        parity = core if which == 0 else 1 - core
        value = jnp.dot(turned, ref[...], preferred_element_type=F32)
        for g in range(2):
            flat[2 * which + g] = value[:, g * 128 : (g + 1) * 128]
        for g in range(2):
            for qc in range(2):
                parts = [
                    flat[2 * which + g, pl.ds(qc * 128 + lo, 32, stride=4), :] for lo in range(4)
                ]
                for t, part in enumerate(chunk_transpose(parts)):
                    where = (2 * (4 * g + t) + parity, pl.ds(4 * qc, 4))
                    out_ref[where] = part.reshape(4, 8, 128).astype(BF16)


def left_kernel(far_ref, gp_ref, keep_ref, got_ref, sum_ref, right_ref, out_ref, flag_ref, raw, gp, prod, out):
    total = half_order(far_ref, raw, gp) + sum_ref[0:1, :]
    flag_ref[0] = (jnp.max(total) > 3e38).astype(jnp.int32)
    high, rest = split_halves(total)
    out[pl.ds(16, 128, stride=18), :] = jnp.broadcast_to(high, (128, 128))
    out[pl.ds(17, 128, stride=18), :] = jnp.broadcast_to(rest, (128, 128))
    value = jnp.dot(gp_ref[...], keep_ref[...], preferred_element_type=F32)
    value += jnp.dot(gp[...], got_ref[...], preferred_element_type=F32)
    for g in range(2):
        prod[g] = value[:, g * 128 : (g + 1) * 128]
    for g in range(2):
        for rc in range(4):
            parts = [prod[g, pl.ds(lo * 128 + rc * 32, 32), :] for lo in range(4)]
            for t, part in enumerate(chunk_transpose(parts)):
                for u in range(4):
                    at = (4 * rc + u) * 8 + 4 * g + t
                    out[pl.ds(at * 18, 8), :] = part[8 * u : 8 * u + 8]
                    out[pl.ds(at * 18 + 8, 8), :] = right_ref[4 * rc + u, 4 * g + t].astype(F32)
    out_ref[...] = out[...].astype(BF16)


VM = pl.BlockSpec(memory_space=pltpu.VMEM)
SM = pl.BlockSpec(memory_space=pltpu.SMEM)


def call(kernel, outs, ins, scratch, name, us=1):
    return pl.pallas_call(
        kernel,
        out_shape=[jax.ShapeDtypeStruct(s, d) for s, d in outs],
        in_specs=ins,
        out_specs=[SM if s == (1,) else VM for s, _ in outs],
        scratch_shapes=[pltpu.VMEM(s, d) for s, d in scratch],
        compiler_params=PARAMS,
        cost_estimate=pl.CostEstimate(flops=0, bytes_accessed=3_000_000 * us, transcendentals=0),
        name=name,
    )


def exchange(x):
    return lax.all_to_all(x, ("row", "col"), 0, 0, axis_index_groups=SAME_CORE, tiled=True)


def other_core(x):
    return lax.ppermute(x, "col", [(i, i ^ 1) for i in range(16)])


def local(left_proj, right_proj, gate, out_weight, grad_out):
    core = (lax.axis_index("col") & 1).astype(jnp.int32).reshape(1)
    sides = jnp.concatenate([left_proj.reshape(1024, 128), right_proj.reshape(1024, 128)])
    (packed,) = call(
        pack_kernel, [((128, 16, 128), BF16)], [SM, VM], [((128, 16, 128), F32)], "pack"
    )(core, sides)
    blocks = exchange(packed).reshape(16, 8, 16, 128)
    (a,) = call(
        left_order_kernel, [((512, 256), BF16)], [VM], [((16, 8, 8, 128), F32)], "left_order"
    )(blocks)
    other = other_core(a)
    keep, send = call(
        right_order_kernel,
        [((256, 256), BF16), ((256, 256), BF16)],
        [SM, VM],
        [((16, 8, 8, 128), F32), ((4, 256, 128), F32)],
        "right_order",
    )(core, blocks)

    def middle(dtype):
        flat = (1024, 128)
        pair, gates, ups, weight = call(
            pair_kernel,
            [((16, 8, 8, 128), F32), (flat, BF16), (flat, BF16), ((128, 128), BF16)],
            [VM] * 7,
            [((2, 512, 128), F32)],
            "pair",
        )(a, other, keep, send, gate.reshape(flat), grad_out.reshape(flat), out_weight)
        got = other_core(send)
        pair, got = lax.optimization_barrier((pair, got))
        pair = exchange(pair.reshape(128, 8, 128).astype(dtype)).astype(F32)
        grad_gate, grad_pair = call(
            functools.partial(norm_kernel, dtype != F32),
            [((1024, 128), BF16), ((1280, 128), BF16)],
            [VM] * 4,
            [((1280, 128), F32)],
            "norm",
        )(pair.reshape(flat), gates, ups, weight)
        own = exchange(grad_pair.reshape(128, 5, 2, 128))
        far = other_core(own)
        half, total, right = call(
            right_kernel,
            [((512, 256), BF16), ((8, 128), F32), ((16, 8, 8, 128), BF16)],
            [SM] + [VM] * 4,
            [((1280, 128), F32), ((4, 256, 128), F32)],
            "right",
        )(core, own.reshape(1280, 128), a, other, grad_gate)
        grads, flag = call(
            left_kernel,
            [((2304, 128), BF16), ((1,), jnp.int32)],
            [VM] * 6,
            [((1280, 128), F32), ((512, 256), BF16), ((2, 512, 128), F32), ((2304, 128), F32)],
            "left",
        )(far.reshape(1280, 128), half, keep, got, total, right)
        grads = exchange(grads.reshape(128, 9, 2, 128))
        grad_left, grad_right, grad_weight = call(
            unpack_kernel,
            [((1024, 128), BF16), ((1024, 128), BF16), ((128, 128), F32)],
            [VM],
            [((2304, 128), F32)],
            "unpack",
        )(grads.reshape(2304, 128))
        return flag[0], (grad_left, grad_right, grad_gate, grad_weight)

    flag, outs = middle(jnp.float16)
    left, right, gates, weight = lax.cond(flag > 0, lambda: middle(F32)[1], lambda: outs)
    shape = (32, 32, 128)
    return left.reshape(shape), right.reshape(shape), gates.reshape(shape), weight


def solution(mesh):
    return jax.shard_map(
        local,
        mesh=mesh,
        in_specs=(
            P("row", "col", None),
            P("col", "row", None),
            P("row", "col", None),
            P(),
            P("row", "col", None),
        ),
        out_specs=(P("row", "col", None), P("col", "row", None), P("row", "col", None), P()),
        check_vma=False,
    )
```

```python
import functools

import jax
import jax.numpy as jnp
from jax import lax
from jax.experimental import pallas as pl
from jax.experimental.pallas import tpu as pltpu
from jax.sharding import PartitionSpec as P

F32 = jnp.float32
BF16 = jnp.bfloat16
PARAMS = pltpu.CompilerParams(vmem_limit_bytes=32 * 1024 * 1024)
NT = (((1,), (1,)), ((), ()))
TN = (((0,), (0,)), ((), ()))
FLOOR = 1e-07

SAME_CORE = [[row * 16 + col for row in range(16) for col in range(core, 16, 2)] for core in (0, 1)]


def chunk_transpose(parts):
    lane = lax.broadcasted_iota(jnp.int32, parts[0].shape, 1)
    low = lane < 64
    even = (lane & 32) == 0
    turn = lambda x, by: pltpu.roll(x, by, 1)
    y0, y1, y2, y3 = parts
    a0 = jnp.where(low, y0, turn(y2, 64))
    a2 = jnp.where(low, turn(y0, 64), y2)
    a1 = jnp.where(low, y1, turn(y3, 64))
    a3 = jnp.where(low, turn(y1, 64), y3)
    return [
        jnp.where(even, a0, turn(a1, 32)),
        jnp.where(even, turn(a0, 96), a1),
        jnp.where(even, a2, turn(a3, 32)),
        jnp.where(even, turn(a2, 96), a3),
    ]


def split_halves(x):
    high = x.astype(BF16).astype(F32)
    return high, (x - high).astype(BF16).astype(F32)


def pack_kernel(core_ref, in_ref, out_ref, slabs):
    for side in range(2):
        for s in range(8):
            slab = in_ref[pl.ds(side * 1024 + s * 128, 128), :].astype(F32)
            slabs[:, side * 8 + s, :] = slab.T
    out_ref[...] = slabs[...].astype(BF16)


def unpack_kernel(in_ref, left_ref, right_ref, weight_ref, slabs):
    slabs[...] = in_ref[...].astype(F32)
    for side, ref in enumerate((left_ref, right_ref)):
        for s in range(8):
            slab = slabs[pl.ds(side * 8 + s, 128, stride=18), :]
            ref[pl.ds(s * 128, 128), :] = slab.T.astype(BF16)
    weight_ref[...] = slabs[pl.ds(16, 128, stride=18), :] + slabs[pl.ds(17, 128, stride=18), :]


def left_order_kernel(in_ref, a_ref, raw):
    raw[...] = in_ref[:, :, 0:8].astype(F32)
    for g in range(2):
        for rc in range(4):
            parts = [raw[pl.ds(4 * rc, 4), 4 * g + t].reshape(32, 128) for t in range(4)]
            for lo, part in enumerate(chunk_transpose(parts)):
                a_ref[pl.ds(lo * 128 + rc * 32, 32), pl.ds(g * 128, 128)] = part.astype(BF16)


def right_order_kernel(core_ref, in_ref, keep_ref, send_ref, raw, nat):
    core = core_ref[0]
    raw[...] = in_ref[:, :, 8:16].astype(F32)
    for which, ref in enumerate((keep_ref, send_ref)):
        parity = core if which == 0 else 1 - core
        for g in range(2):
            for qc in range(2):
                parts = [
                    raw[2 * (4 * g + t) + parity, pl.ds(4 * qc, 4)].reshape(32, 128)
                    for t in range(4)
                ]
                for lo, part in enumerate(chunk_transpose(parts)):
                    nat[2 * which + g, pl.ds(qc * 128 + lo, 32, stride=4), :] = part
            ref[:, pl.ds(g * 128, 128)] = nat[2 * which + g].astype(BF16)


def pair_kernel(a_ref, other_ref, keep_ref, send_ref, gate_ref, grad_ref, weight_ref, out_ref, gate_out, grad_out, weight_out, prod):
    weight_out[...] = weight_ref[...]
    gate_out[...] = gate_ref[...]
    grad_out[...] = grad_ref[...]
    value = lax.dot_general(a_ref[...], keep_ref[...], NT, preferred_element_type=F32)
    value += lax.dot_general(other_ref[...], send_ref[...], NT, preferred_element_type=F32)
    for g in range(2):
        prod[g] = value[:, g * 128 : (g + 1) * 128]
    for g in range(2):
        for rc in range(4):
            parts = [prod[g, pl.ds(lo * 128 + rc * 32, 32), :] for lo in range(4)]
            for t, part in enumerate(chunk_transpose(parts)):
                out_ref[pl.ds(4 * rc, 4), 4 * g + t] = part.reshape(4, 8, 128)


def norm_kernel(rounded, pair_ref, gate_ref, grad_ref, weight_ref, gate_out, out_ref, slabs):
    worst = jnp.full((1, 128), -1.0, F32)
    weight = weight_ref[...]
    total = jnp.zeros((128, 128), F32)
    for s in range(8):
        rows = pl.ds(s * 128, 128)
        pair = pair_ref[pl.ds(s, 128, stride=8), :]
        average = jnp.mean(pair, axis=0, keepdims=True)
        centered = pair - average
        variance = jnp.mean(centered * centered, axis=0, keepdims=True)
        inv_std = lax.rsqrt(variance + 1e-05)
        worst = jnp.maximum(worst, average * average + FLOOR - variance)
        normed = centered * inv_std
        normed_half = normed.astype(BF16)
        gate_prob = jax.nn.sigmoid(gate_ref[rows, :].astype(F32))
        upstream = grad_ref[rows, :].astype(F32)
        gated = upstream * gate_prob
        gated_grad = gated.astype(BF16)
        projected = lax.dot_general(normed_half, weight, TN, preferred_element_type=F32)
        gate_out[rows, :] = (gated * projected * (1.0 - gate_prob)).astype(BF16)
        total += jnp.dot(normed_half, gated_grad, preferred_element_type=F32)
        grad_normed = lax.dot_general(weight, gated_grad, NT, preferred_element_type=F32)
        mean_one = jnp.mean(grad_normed, axis=0, keepdims=True)
        mean_two = jnp.mean(grad_normed * normed, axis=0, keepdims=True)
        grad_pair = (grad_normed - mean_one - normed * mean_two) * inv_std
        slabs[pl.ds(s, 128, stride=10), :] = grad_pair
    high, rest = split_halves(total * (1.0 / 512.0))
    if rounded:
        high = jnp.where(jnp.max(worst, axis=1, keepdims=True) > 0.0, jnp.inf, high)
    slabs[pl.ds(8, 128, stride=10), :] = high
    slabs[pl.ds(9, 128, stride=10), :] = rest
    out_ref[...] = slabs[...].astype(BF16)


def half_order(ref, raw, gp):
    raw[...] = ref[...].astype(F32)
    for g in range(2):
        for rc in range(4):
            parts = [
                jnp.concatenate(
                    [raw[pl.ds((8 * r + 4 * g + t) * 10, 8), :] for r in range(4 * rc, 4 * rc + 4)]
                )
                for t in range(4)
            ]
            for lo, part in enumerate(chunk_transpose(parts)):
                gp[pl.ds(lo * 128 + rc * 32, 32), pl.ds(g * 128, 128)] = part.astype(BF16)
    terms = [raw[pl.ds(8 + row, 128, stride=10), :] for row in range(2)]
    return jnp.sum(terms[0], axis=0, keepdims=True) + jnp.sum(terms[1], axis=0, keepdims=True)


def right_kernel(core_ref, own_ref, a_ref, other_ref, gate_ref, keep_ref, gp_ref, sum_ref, out_ref, near_ref, raw, flat):
    core = core_ref[0]
    sum_ref[...] = jnp.broadcast_to(half_order(own_ref, raw, gp_ref), (8, 128))
    near_ref[...] = jnp.dot(gp_ref[...], keep_ref[...], preferred_element_type=F32)
    turned = gp_ref[...].T
    for which, ref in enumerate((a_ref, other_ref)):
        parity = core if which == 0 else 1 - core
        value = jnp.dot(turned, ref[...], preferred_element_type=F32)
        for g in range(2):
            flat[2 * which + g] = value[:, g * 128 : (g + 1) * 128]
        for g in range(2):
            for qc in range(2):
                parts = [
                    flat[2 * which + g, pl.ds(qc * 128 + lo, 32, stride=4), :] for lo in range(4)
                ]
                for t, part in enumerate(chunk_transpose(parts)):
                    where = (2 * (4 * g + t) + parity, pl.ds(4 * qc, 4))
                    out_ref[where] = part.reshape(4, 8, 128).astype(BF16)


def left_kernel(far_ref, near_ref, got_ref, sum_ref, right_ref, out_ref, flag_ref, raw, gp, prod, out):
    total = half_order(far_ref, raw, gp) + sum_ref[0:1, :]
    flag_ref[0] = (jnp.max(total) > 3e38).astype(jnp.int32)
    high, rest = split_halves(total)
    out[pl.ds(16, 128, stride=18), :] = jnp.broadcast_to(high, (128, 128))
    out[pl.ds(17, 128, stride=18), :] = jnp.broadcast_to(rest, (128, 128))
    value = near_ref[...] + jnp.dot(gp[...], got_ref[...], preferred_element_type=F32)
    for g in range(2):
        prod[g] = value[:, g * 128 : (g + 1) * 128]
    for g in range(2):
        for rc in range(4):
            parts = [prod[g, pl.ds(lo * 128 + rc * 32, 32), :] for lo in range(4)]
            for t, part in enumerate(chunk_transpose(parts)):
                for u in range(4):
                    at = (4 * rc + u) * 8 + 4 * g + t
                    out[pl.ds(at * 18, 8), :] = part[8 * u : 8 * u + 8]
                    out[pl.ds(at * 18 + 8, 8), :] = right_ref[4 * rc + u, 4 * g + t].astype(F32)
    out_ref[...] = out[...].astype(BF16)


VM = pl.BlockSpec(memory_space=pltpu.VMEM)
SM = pl.BlockSpec(memory_space=pltpu.SMEM)


def call(kernel, outs, ins, scratch, name, us=1):
    return pl.pallas_call(
        kernel,
        out_shape=[jax.ShapeDtypeStruct(s, d) for s, d in outs],
        in_specs=ins,
        out_specs=[SM if s == (1,) else VM for s, _ in outs],
        scratch_shapes=[pltpu.VMEM(s, d) for s, d in scratch],
        compiler_params=PARAMS,
        cost_estimate=pl.CostEstimate(flops=0, bytes_accessed=3_000_000 * us, transcendentals=0),
        name=name,
    )


def exchange(x):
    return lax.all_to_all(x, ("row", "col"), 0, 0, axis_index_groups=SAME_CORE, tiled=True)


def other_core(x):
    return lax.ppermute(x, "col", [(i, i ^ 1) for i in range(16)])


def local(left_proj, right_proj, gate, out_weight, grad_out):
    core = (lax.axis_index("col") & 1).astype(jnp.int32).reshape(1)
    sides = jnp.concatenate([left_proj.reshape(1024, 128), right_proj.reshape(1024, 128)])
    (packed,) = call(
        pack_kernel, [((128, 16, 128), BF16)], [SM, VM], [((128, 16, 128), F32)], "pack"
    )(core, sides)
    blocks = exchange(packed).reshape(16, 8, 16, 128)
    (a,) = call(
        left_order_kernel, [((512, 256), BF16)], [VM], [((16, 8, 8, 128), F32)], "left_order"
    )(blocks)
    other = other_core(a)
    keep, send = call(
        right_order_kernel,
        [((256, 256), BF16), ((256, 256), BF16)],
        [SM, VM],
        [((16, 8, 8, 128), F32), ((4, 256, 128), F32)],
        "right_order",
    )(core, blocks)

    def middle(dtype):
        flat = (1024, 128)
        pair, gates, ups, weight = call(
            pair_kernel,
            [((16, 8, 8, 128), F32), (flat, BF16), (flat, BF16), ((128, 128), BF16)],
            [VM] * 7,
            [((2, 512, 128), F32)],
            "pair",
        )(a, other, keep, send, gate.reshape(flat), grad_out.reshape(flat), out_weight)
        got = other_core(send)
        pair, got = lax.optimization_barrier((pair, got))
        pair = exchange(pair.reshape(128, 8, 128).astype(dtype)).astype(F32)
        grad_gate, grad_pair = call(
            functools.partial(norm_kernel, dtype != F32),
            [((1024, 128), BF16), ((1280, 128), BF16)],
            [VM] * 4,
            [((1280, 128), F32)],
            "norm",
        )(pair.reshape(flat), gates, ups, weight)
        own = exchange(grad_pair.reshape(128, 5, 2, 128))
        far = other_core(own)
        _, total, right, near = call(
            right_kernel,
            [((512, 256), BF16), ((8, 128), F32), ((16, 8, 8, 128), BF16), ((512, 256), F32)],
            [SM] + [VM] * 5,
            [((1280, 128), F32), ((4, 256, 128), F32)],
            "right",
        )(core, own.reshape(1280, 128), a, other, grad_gate, keep)
        grads, flag = call(
            left_kernel,
            [((2304, 128), BF16), ((1,), jnp.int32)],
            [VM] * 5,
            [((1280, 128), F32), ((512, 256), BF16), ((2, 512, 128), F32), ((2304, 128), F32)],
            "left",
        )(far.reshape(1280, 128), near, got, total, right)
        grads = exchange(grads.reshape(128, 9, 2, 128))
        grad_left, grad_right, grad_weight = call(
            unpack_kernel,
            [((1024, 128), BF16), ((1024, 128), BF16), ((128, 128), F32)],
            [VM],
            [((2304, 128), F32)],
            "unpack",
        )(grads.reshape(2304, 128))
        return flag[0], (grad_left, grad_right, grad_gate, grad_weight)

    flag, outs = middle(jnp.float16)
    left, right, gates, weight = lax.cond(flag > 0, lambda: middle(F32)[1], lambda: outs)
    shape = (32, 32, 128)
    return left.reshape(shape), right.reshape(shape), gates.reshape(shape), weight


def solution(mesh):
    return jax.shard_map(
        local,
        mesh=mesh,
        in_specs=(
            P("row", "col", None),
            P("col", "row", None),
            P("row", "col", None),
            P(),
            P("row", "col", None),
        ),
        out_specs=(P("row", "col", None), P("col", "row", None), P("row", "col", None), P()),
        check_vma=False,
    )
```
